32 devices in a mesh: slab: 16 (over z, x, core), shell: 2 (over y).
Axes of the slice: x: 2, y: 2, z: 4, core: 2. Of those that a mesh axis runs over, the one named last changes fastest.
Arguments:
- images: bfloat16 [2048, 2, 16384], P('slab', None, 'shell'), may hold values from -6 to 6
- defocus: bfloat16 [2048], P('slab'), may hold values from 20 to 200
- pose_bin: int32 [2048, 1], P('slab'), may hold values from 0 to 15; in each aligned block of 128 rows (0 to 127, 128 to 255, ...) at most 24 rows name the same one
- freq_sq: float32 [16384], P('shell'), may hold values from 0 to 1, as said below
- model_slice: float32 [16, 2, 16384], P('slab', None, 'shell'), may hold values from -6 to 6
- interp_coef: bfloat16 [16, 128, 4, 128, 128], P('slab', 'shell'), may hold values from -0.5 to 0.5
- block_index: int32 [16, 128, 4], P('slab', 'shell'), may hold values from 0 to 127, as said below
Outputs:
- volume_grad: float32 [128, 2, 128], P(('slab', 'shell'))
The draws below stay inside these ranges and needn't reach their ends.
Inputs may be any that keep to these rules, and one draw needn't show every extreme that they name: `pose_bin`: among the images of one index of slab, no pose bin is named by more than 24 images, a bound that some block reaches. `freq_sq`: band s of the 2 bands of samples holds values between (s / 2) squared and ((s + 1) / 2) squared. `block_index`: among the 256 dense blocks of one pose bin in one shell band, the volume blocks v with the same v // 8 are named at most 32 times, and one such group exactly 32 times.
All inputs are finite; a program needn't handle non-finite values.
Results may differ from the reference program's by a relative error of at most 0.0029.
Values may be sent and summed in bfloat16 or wider, within the bound.
No kernel may reach another device: no remote copies, remote signals or barrier semaphores. Data moves between devices by JAX's collectives and lax.ppermute only.
A program may use at most 64 MiB of HBM per device.

```python
import math
import jax
import jax.numpy as jnp
import numpy as np
from jax import lax

IMG_DEV = 128
NVB_DEV = 4
PIX = 16384
PB = 128
VB = 128
NNZ = 4
IMAGES = 2048
BINS = 16
BANDS = 2
CAP = 24
KB = 128
KBD = 64
TERMS = 256
CAPV = 32
NV = 128
N_SLAB = 16


def draw_freq_sq(key, part):
    width = PIX // BANDS
    band = (jnp.arange(PIX, dtype=jnp.int32) // width).astype(jnp.float32)
    unit = jax.random.uniform(jax.random.fold_in(key, 11), (PIX,), jnp.float32)
    radius = (band + unit) / BANDS
    return jnp.clip(radius * radius, 0.0, 1.0)


def one_group(key):
    keys = jax.random.split(key, 4)
    group = NVB_DEV * BANDS
    first = jax.random.randint(keys[0], (), 0, N_SLAB)
    slots = jax.random.permutation(keys[1], (N_SLAB - 1) * CAPV)
    others = slots // CAPV
    others = others + (others >= first).astype(jnp.int32)
    owners = jnp.concatenate([jnp.full((CAPV,), first, jnp.int32), others[:TERMS - CAPV].astype(jnp.int32)])
    order = jax.random.permutation(keys[2], TERMS)
    owners = owners[order]
    local_block = jax.random.randint(keys[3], (TERMS,), 0, group)
    return (owners * group + local_block).astype(jnp.int32).reshape(KBD, NNZ)


def draw_block_index(key, part):
    base = jax.random.fold_in(key, 29)
    keys = jax.vmap(lambda n: jax.random.fold_in(base, n))(jnp.arange(BINS * BANDS, dtype=jnp.int32))
    blocks = jax.vmap(one_group)(keys)
    return blocks.reshape(BINS, KB, NNZ)


def steps_of(rng, shape, cuts, smallest, top_value):
    def one(dim, shards_of):
        heights = jax.random.uniform(jax.random.fold_in(jax.random.fold_in(rng, 6), dim), (shards_of,), jnp.float32, smallest / len(cuts), top_value / len(cuts))
        return jnp.repeat(jnp.exp(heights), shape[dim] // shards_of).reshape((-1,) + (1,) * (len(shape) - dim - 1))

    factor_of = one(*cuts[0])
    for cut in cuts[1:]:
        factor_of = factor_of * one(*cut)
    return factor_of


def shared_out(key, own, number, rows, number_of, top, limit, lean):
    order = jax.random.permutation(key, number_of)
    heavy_load, common = shares(number_of, rows * top, limit, lean, True), shares(number_of, rows * top, limit, lean, False)
    places = jnp.arange(number_of)

    def named(tallies, offset_by):
        used = int((tallies > 0).sum())
        fixed = max(1, used // 4)
        moved = fixed + (places - fixed + offset_by * (used - fixed)) % max(1, number_of - fixed)
        return jnp.zeros((number_of,), jnp.int32).at[order[jnp.where(places < fixed, places, moved)]].set(jnp.asarray(tallies, jnp.int32))

    tallies = jnp.where(number % 4 == 0, named(heavy_load, number // 4), named(common, number - number // 4 - 1))
    mixed = jax.random.permutation(jax.random.fold_in(own, 3), number_of)
    giver, receiver = mixed[0:number_of // 2 * 2:2], mixed[1:number_of // 2 * 2:2]
    room = jnp.minimum(tallies[giver] - 1, limit - tallies[receiver]) // 2
    room = jnp.where((giver == order[0]) | (receiver == order[0]) | (tallies[receiver] == 0), 0, jnp.maximum(room, 0))
    moved = jax.random.randint(jax.random.fold_in(own, 4), (number_of // 2,), 0, 1 << 20) % (room + 1)
    tallies = tallies.at[giver].add(-moved).at[receiver].add(moved)
    items = jnp.searchsorted(jnp.cumsum(tallies), jnp.arange(rows * top), side="right").astype(jnp.int32)
    table = items.reshape(top, rows).T
    table = table[jax.random.permutation(jax.random.fold_in(own, 1), rows)]
    offset_by = jax.random.randint(jax.random.fold_in(own, 2), (rows, 1), 0, top)
    return jnp.take_along_axis(table, (jnp.arange(top)[None, :] + offset_by) % top, axis=1)


def shares(amount, total, reach, skew, full):
    portions = [(1 << 20) // math.isqrt(standing ** skew) + 1 for standing in range(1, amount + 1)]
    largest = reach if full else min(reach, max(-(-total // amount), total * portions[0] // sum(portions)))
    least = 1 if total - largest >= amount - 1 else 0
    holding, surplus = [largest] + [least] * (amount - 1), total - largest - least * (amount - 1)
    while surplus > 0:
        candidates = [i for i in range(1, amount) if holding[i] < largest] or [i for i in range(1, amount) if holding[i] < reach]
        mass, left = sum([portions[i] for i in candidates]), surplus
        for i in candidates:
            addition = min(reach - holding[i], max(1, left * portions[i] // mass), surplus)
            holding[i] = holding[i] + addition
            surplus = surplus - addition
    return np.array(holding)


def centred(rng, dims, deviation, reach, cuts=(), kind=jnp.bfloat16):
    gain = steps_of(rng, dims, cuts, -0.22, 0.18) if cuts else 1.0
    values = jax.random.normal(rng, dims, jnp.float32) * deviation * gain
    return jnp.minimum(jnp.maximum(values, -reach), reach).astype(kind)


def setup_inputs(seed: int = 0) -> dict:
    seeds = jax.random.split(jax.random.key(seed), 8)
    images = centred(seeds[0], (IMAGES, 2, PIX), 1.0, 6.0, ((0, 16), (2, 2)))
    defocus = jnp.clip(jnp.exp(math.log(200.0) - 2.3025851 * jax.random.uniform(seeds[1], (IMAGES,), jnp.float32) ** steps_of(seeds[1], (IMAGES,), ((0, 16),), -0.2, 0.2)), 20.0, 200.0).astype(jnp.bfloat16)
    pose_bin_keys = jax.random.split(jax.random.fold_in(seeds[2], 1), IMAGES // IMG_DEV)
    pose_bin_turns = jax.random.permutation(jax.random.fold_in(seeds[2], 3), IMAGES // IMG_DEV)
    pose_bin = jax.vmap(lambda own, number: shared_out(jax.random.fold_in(seeds[2], 2), own, number, IMG_DEV, BINS, 1, CAP, 2))(pose_bin_keys, pose_bin_turns).reshape((IMAGES, 1))
    freq_sq = draw_freq_sq(jax.random.fold_in(seeds[7], 71), 0)
    model_slice = centred(seeds[4], (BINS, 2, PIX), 1.0, 6.0, ((0, 16), (2, 2)), jnp.float32)
    interp_coef = centred(seeds[5], (BINS, KB, NNZ, PB, VB), PB ** -0.5, 0.5, ((0, 16), (1, 2)))
    block_index = draw_block_index(jax.random.fold_in(seeds[7], 71), 0)
    return dict(images=images, defocus=defocus, pose_bin=pose_bin, freq_sq=freq_sq, model_slice=model_slice, interp_coef=interp_coef, block_index=block_index)


def reference(images, defocus, pose_bin, freq_sq, model_slice, interp_coef, block_index):
    f32 = jnp.float32
    bin_ids = jnp.arange(BINS, dtype=jnp.int32)

    def accumulate(carry, which):
        numerator, power = carry
        start = which.astype(jnp.int32) * IMG_DEV
        rows = lax.dynamic_slice_in_dim(images, start, IMG_DEV, 0).astype(f32)
        focus = lax.dynamic_slice_in_dim(defocus, start, IMG_DEV, 0).astype(f32)
        labels = lax.dynamic_slice_in_dim(pose_bin, start, IMG_DEV, 0)[:, 0]
        onehot = (labels[:, None] == bin_ids[None, :]).astype(f32)
        contrast = jnp.sin(focus[:, None] * freq_sq[None, :])
        numerator = numerator + jnp.einsum("ib,ics->bcs", onehot, contrast[:, None, :] * rows, precision=lax.Precision.HIGHEST)
        power = power + jnp.dot(onehot.T, contrast * contrast, precision=lax.Precision.HIGHEST)
        return (numerator, power), None

    start_carry = (jnp.zeros((BINS, 2, PIX), f32), jnp.zeros((BINS, PIX), f32))
    (numerator, power), _ = lax.scan(accumulate, start_carry, jnp.arange(N_SLAB, dtype=jnp.int32))
    residual_slice = ((power[:, None, :] * model_slice - numerator) / IMG_DEV).astype(jnp.bfloat16)

    def insert(grad, pieces):
        slice_one, coef_one, index_one = pieces
        tiles = slice_one.reshape(2, KB, PB).astype(f32)
        terms = jnp.einsum("ckp,kjpv->kjcv", tiles, coef_one.astype(f32), precision=lax.Precision.HIGHEST)
        grad = grad.at[index_one.reshape(-1)].add(terms.reshape(-1, 2, VB))
        return grad, None

    volume_grad, _ = lax.scan(insert, jnp.zeros((NV, 2, VB), f32), (residual_slice, interp_coef, block_index))
    return volume_grad
```

```python
import functools
import math

import jax
import jax.numpy as jnp
import numpy as np
from jax import lax
from jax.experimental import pallas as pl
from jax.experimental.pallas import tpu as pltpu
from jax.sharding import PartitionSpec as P

f32 = jnp.float32
bf16 = jnp.bfloat16
LANES = 128
GROUP = 8
ROUND = 12582912.0


def sine_coefficients():
    x = np.cos(np.pi * (np.arange(400) + 0.5) / 400)
    cheb = np.polynomial.chebyshev.Chebyshev.fit(x, np.sin(np.pi * x), 11, domain=[-1, 1])
    power = cheb.convert(kind=np.polynomial.Polynomial).coef
    return [float(power[2 * n + 1] * 2.0 ** (2 * n + 1)) for n in range(6)]


SINE = sine_coefficients()


def sine_of_turns(turns):
    r = turns - ((turns + ROUND) - ROUND)
    q = r * r
    s = q * SINE[5] + SINE[4]
    for n in (3, 2, 1, 0):
        s = s * q + SINE[n]
    return s * r


def sums_kernel(
    blocks, half, pose_ref, images_ref, defocus_ref, freq_ref, mine_ref, other_ref, acc, turns, spread
):
    step = pl.program_id(0)
    chunk = images_ref.shape[0]

    @pl.when(step == 0)
    def _():
        acc[...] = jnp.zeros_like(acc)
        turns[...] = freq_ref[...] * (0.5 / math.pi)
        n = defocus_ref.shape[1]
        rows = lax.broadcasted_iota(jnp.int32, (n, n), 0)
        cols = lax.broadcasted_iota(jnp.int32, (n, n), 1)
        diagonal = jnp.where(rows == cols, defocus_ref[...].astype(f32), 0.0).astype(bf16)
        spread[...] = jnp.dot(diagonal, jnp.ones((n, LANES), bf16), preferred_element_type=f32)

    side = lax.axis_index("slab") & 1
    rows = lax.broadcasted_iota(jnp.int32, (2 * blocks, 2 * blocks), 0)
    cols = lax.broadcasted_iota(jnp.int32, (2 * blocks, 2 * blocks), 1)
    apart = jnp.where(cols == 2 * (rows % blocks) + rows // blocks, 1.0, 0.0).astype(bf16)

    def one(i):
        image = step * chunk + i
        s = sine_of_turns(spread[pl.ds(image, 1), :] * turns[...])
        both = jnp.dot(apart, images_ref[i], preferred_element_type=f32)
        pose = pose_ref[image]
        slot = ((pose & 1) ^ side) * half + (pose >> 1)
        return slot, s, both

    def body(j, _):
        done = [one(2 * j + k) for k in range(2)]
        for slot, s, both in done:
            acc[slot, :blocks] += s * both[:blocks]
            acc[slot, blocks : 2 * blocks] += s * both[blocks:]
            acc[slot, 2 * blocks :] += s * s
        return 0

    lax.fori_loop(0, chunk // 2, body, 0)

    @pl.when(step == pl.num_programs(0) - 1)
    def _():
        mine_ref[...] = acc[:half]
        other_ref[...] = acc[half:]


def weighted_sums(images, defocus, pose_bin, freq_sq, bins):
    count, _, width = images.shape
    blocks = width // LANES
    half = bins // 2
    chunk = 16
    rows = images.reshape(count, 2, blocks, LANES).transpose(0, 2, 1, 3).reshape(count, 2 * blocks, LANES)
    part = jax.ShapeDtypeStruct((half, 3 * blocks, LANES), f32)
    whole = pl.BlockSpec((half, 3 * blocks, LANES), lambda i, p: (0, 0, 0))
    return pl.pallas_call(
        functools.partial(sums_kernel, blocks, half),
        grid_spec=pltpu.PrefetchScalarGridSpec(
            num_scalar_prefetch=1,
            grid=(count // chunk,),
            in_specs=[
                pl.BlockSpec((chunk, 2 * blocks, LANES), lambda i, p: (i, 0, 0)),
                pl.BlockSpec((1, count), lambda i, p: (0, 0)),
                pl.BlockSpec((blocks, LANES), lambda i, p: (0, 0)),
            ],
            out_specs=[whole, whole],
            scratch_shapes=[
                pltpu.VMEM((bins, 3 * blocks, LANES), f32),
                pltpu.VMEM((blocks, LANES), f32),
                pltpu.VMEM((count, LANES), f32),
            ],
        ),
        out_shape=[part, part],
        compiler_params=pltpu.CompilerParams(vmem_limit_bytes=24 * 2**20),
    )(pose_bin.reshape(-1), rows, defocus.reshape(1, -1), freq_sq.reshape(blocks, LANES))


def volume_kernel(blocks, scale, sums_ref, model_ref, index_ref, coef_ref, out_ref, residual, terms):
    step = pl.program_id(0)
    touched = coef_ref.shape[1]

    @pl.when(step == 0)
    def _():
        total = jnp.sum(sums_ref[...].astype(f32), axis=0)
        power = total[2 * blocks :]
        for c in range(2):
            model = model_ref[pl.ds(c, blocks, 2), :]
            residual[c] = (power * model - total[c * blocks : (c + 1) * blocks]) * scale

    first = pl.multiple_of(step * GROUP, GROUP)
    row = lax.broadcasted_iota(jnp.int32, (GROUP, LANES), 0)
    left = jnp.concatenate(
        [
            jnp.concatenate(
                [jnp.where(row == m, residual[c, pl.ds(first, GROUP), :], 0.0) for m in range(GROUP)],
                axis=1,
            )
            for c in range(2)
        ],
        axis=0,
    ).astype(bf16)
    for j in range(touched):
        right = coef_ref[:, j].reshape(GROUP * LANES, LANES)
        got = jnp.dot(left, right, preferred_element_type=f32)
        for c in range(2):
            terms[j, pl.ds(first, GROUP), c * LANES : (c + 1) * LANES] = got[c * GROUP : (c + 1) * GROUP]

    @pl.when(step == pl.num_programs(0) - 1)
    def _():
        volume = out_ref.shape[0]
        rows = lax.broadcasted_iota(jnp.int32, (volume, blocks), 0)
        total = jnp.zeros(out_ref.shape, f32)
        for j in range(touched):
            onehot = jnp.where(rows == index_ref[pl.ds(j, 1), :], 1.0, 0.0).astype(bf16)
            whole = terms[j]
            for _ in range(3):
                piece = whole.astype(bf16)
                whole = whole - piece.astype(f32)
                total = total + jnp.dot(onehot, piece, preferred_element_type=f32)
        out_ref[...] = total


def volume_share(sums, model_slice, interp_coef, block_index, volume, scale):
    parts = sums.shape[0]
    _, blocks, touched, _, _ = interp_coef.shape
    model = model_slice.reshape(2, blocks, LANES).transpose(1, 0, 2).reshape(2 * blocks, LANES)
    return pl.pallas_call(
        functools.partial(volume_kernel, blocks, scale),
        grid=(blocks // GROUP,),
        in_specs=[
            pl.BlockSpec((parts, 3 * blocks, LANES), lambda i: (0, 0, 0)),
            pl.BlockSpec((2 * blocks, LANES), lambda i: (0, 0)),
            pl.BlockSpec((touched, blocks), lambda i: (0, 0)),
            pl.BlockSpec((GROUP, touched, LANES, LANES), lambda i: (i, 0, 0, 0)),
        ],
        out_specs=pl.BlockSpec((volume, 2 * LANES), lambda i: (0, 0)),
        out_shape=jax.ShapeDtypeStruct((volume, 2 * LANES), f32),
        scratch_shapes=[
            pltpu.VMEM((2, blocks, LANES), f32),
            pltpu.VMEM((touched, blocks, 2 * LANES), f32),
        ],
        compiler_params=pltpu.CompilerParams(vmem_limit_bytes=24 * 2**20),
    )(sums, model, block_index[0].T, interp_coef[0])


def shards(images, defocus, pose_bin, freq_sq, model_slice, interp_coef, block_index, volume):
    slabs = lax.axis_size("slab")
    shells = lax.axis_size("shell")
    mine, other = weighted_sums(images, defocus, pose_bin, freq_sq, slabs)
    other = lax.ppermute(other, "slab", [(i, i ^ 1) for i in range(slabs)])
    pair = (mine + other).astype(bf16)
    sums = lax.all_to_all(
        pair,
        "slab",
        split_axis=0,
        concat_axis=0,
        tiled=True,
        axis_index_groups=[list(range(side, slabs, 2)) for side in range(2)],
    )
    share = volume_share(sums, model_slice, interp_coef, block_index, volume, 1.0 / images.shape[0])
    owned = volume // (slabs * shells)
    shares = lax.all_to_all(share, ("slab", "shell"), split_axis=0, concat_axis=0, tiled=True)
    return jnp.sum(shares.reshape(slabs * shells, owned, 2, LANES), axis=0)


def solution(mesh):
    owned = 4
    volume = owned * mesh.shape["slab"] * mesh.shape["shell"]
    return jax.shard_map(
        functools.partial(shards, volume=volume),
        mesh=mesh,
        in_specs=(
            P("slab", None, "shell"),
            P("slab"),
            P("slab", None),
            P("shell"),
            P("slab", None, "shell"),
            P("slab", "shell", None, None, None),
            P("slab", "shell", None),
        ),
        out_specs=P(("slab", "shell"), None, None),
        check_vma=False,
    )
```

```python
import functools
import math

import jax
import jax.numpy as jnp
import numpy as np
from jax import lax
from jax.experimental import pallas as pl
from jax.experimental.pallas import tpu as pltpu
from jax.sharding import PartitionSpec as P

f32 = jnp.float32
bf16 = jnp.bfloat16
LANES = 128
GROUP = 8
ROUND = 12582912.0


def sine_coefficients():
    x = np.cos(np.pi * (np.arange(400) + 0.5) / 400)
    cheb = np.polynomial.chebyshev.Chebyshev.fit(x, np.sin(np.pi * x), 11, domain=[-1, 1])
    power = cheb.convert(kind=np.polynomial.Polynomial).coef
    return [float(power[2 * n + 1] * 2.0 ** (2 * n + 1)) for n in range(6)]


SINE = sine_coefficients()


def sine_of_turns(turns):
    r = turns - ((turns + ROUND) - ROUND)
    q = r * r
    s = q * SINE[5] + SINE[4]
    for n in (3, 2, 1, 0):
        s = s * q + SINE[n]
    return s * r


def sums_kernel(
    half,
    unroll,
    pose_hbm,
    images_hbm,
    defocus_hbm,
    freq_hbm,
    model_hbm,
    index_hbm,
    coef_hbm,
    acc,
    other_ref,
    model_out,
    index_out,
    coef_out,
    pose,
    images,
    defocus,
    turns,
    spread,
    small_sems,
    image_sems,
    late_sems,
):
    count = images.shape[0]
    blocks = turns.shape[0]
    small = [
        pltpu.make_async_copy(src, dst, small_sems.at[n])
        for n, (src, dst) in enumerate(((pose_hbm, pose), (defocus_hbm, defocus), (freq_hbm, turns)))
    ]
    for copy in small:
        copy.start()

    def image_copy(j):
        rows = pl.ds(j * unroll, unroll)
        return pltpu.make_async_copy(images_hbm.at[rows], images.at[rows], image_sems.at[j])

    for j in range(count // unroll):
        image_copy(j).start()
    late = [
        pltpu.make_async_copy(src, dst, late_sems.at[n])
        for n, (src, dst) in enumerate(
            ((model_hbm, model_out), (index_hbm, index_out), (coef_hbm, coef_out))
        )
    ]
    for copy in late:
        copy.start()

    acc[...] = jnp.zeros_like(acc)
    rows = lax.broadcasted_iota(jnp.int32, (2 * blocks, 2 * blocks), 0)
    cols = lax.broadcasted_iota(jnp.int32, (2 * blocks, 2 * blocks), 1)
    apart = jnp.where(cols == 2 * (rows % blocks) + rows // blocks, 1.0, 0.0).astype(bf16)
    rows = lax.broadcasted_iota(jnp.int32, (count, count), 0)
    cols = lax.broadcasted_iota(jnp.int32, (count, count), 1)
    for copy in small:
        copy.wait()
    diagonal = jnp.where(rows == cols, defocus[...].astype(f32), 0.0).astype(bf16)
    spread[...] = jnp.dot(diagonal, jnp.ones((count, LANES), bf16), preferred_element_type=f32)
    turns[...] = turns[...] * (0.5 / math.pi)
    side = lax.axis_index("slab") & 1

    def one(image):
        s = sine_of_turns(spread[pl.ds(image, 1), :] * turns[...])
        both = jnp.dot(apart, images[image], preferred_element_type=f32)
        bin_ = pose[image]
        slot = ((bin_ & 1) ^ side) * half + (bin_ >> 1)
        return slot, s, both

    def body(j, _):
        image_copy(j).wait()
        for slot, s, both in [one(unroll * j + k) for k in range(unroll)]:
            old = acc[slot]
            acc[slot] = old + jnp.concatenate([s * both[:blocks], s * both[blocks:], s * s], axis=0)
        return 0

    lax.fori_loop(0, count // unroll, body, 0)
    other_ref[...] = acc[half:].astype(other_ref.dtype)
    for copy in late:
        copy.wait()


def weighted_sums(images, defocus, pose_bin, freq_sq, model_slice, interp_coef, block_index, bins):
    count, _, width = images.shape
    blocks = width // LANES
    half = bins // 2
    unroll = 16
    rows = images.reshape(count, 2, blocks, LANES).transpose(0, 2, 1, 3).reshape(count, 2 * blocks, LANES)
    model = model_slice.reshape(2, blocks, LANES).transpose(1, 0, 2).reshape(2 * blocks, LANES)
    index = block_index[0].T
    coef = interp_coef[0]
    hbm = pl.BlockSpec(memory_space=pltpu.HBM)
    vmem = pl.BlockSpec(memory_space=pltpu.VMEM)
    shapes = [
        ((bins, 3 * blocks, LANES), f32),
        ((half, 3 * blocks, LANES), bf16),
        (model.shape, f32),
        (index.shape, jnp.int32),
        (coef.shape, bf16),
    ]
    return pl.pallas_call(
        functools.partial(sums_kernel, half, unroll),
        in_specs=[hbm] * 7,
        out_specs=[vmem] * 5,
        out_shape=[jax.ShapeDtypeStruct(shape, dtype) for shape, dtype in shapes],
        scratch_shapes=[
            pltpu.SMEM((count,), jnp.int32),
            pltpu.VMEM(rows.shape, bf16),
            pltpu.VMEM((1, count), bf16),
            pltpu.VMEM((blocks, LANES), f32),
            pltpu.VMEM((count, LANES), f32),
            pltpu.SemaphoreType.DMA((3,)),
            pltpu.SemaphoreType.DMA((count // unroll,)),
            pltpu.SemaphoreType.DMA((3,)),
        ],
        compiler_params=pltpu.CompilerParams(vmem_limit_bytes=24 * 2**20),
    )(*[pltpu.with_memory_space_constraint(a, pltpu.HBM) for a in (pose_bin.reshape(-1), rows, defocus.reshape(1, -1), freq_sq.reshape(blocks, LANES), model, index, coef)])


def volume_kernel(scale, sums_ref, model_ref, index_ref, coef_ref, out_ref, residual, terms):
    blocks, touched = coef_ref.shape[:2]
    total = sums_ref[0].astype(f32)
    for part in range(1, sums_ref.shape[0]):
        total = total + sums_ref[part].astype(f32)
    power = total[2 * blocks :]
    for c in range(2):
        model = model_ref[pl.ds(c, blocks, 2), :]
        residual[c] = (power * model - total[c * blocks : (c + 1) * blocks]) * scale

    row = lax.broadcasted_iota(jnp.int32, (GROUP, LANES), 0)
    for first in range(0, blocks, GROUP):
        left = jnp.concatenate(
            [
                jnp.concatenate(
                    [jnp.where(row == m, residual[c, first : first + GROUP], 0.0) for m in range(GROUP)],
                    axis=1,
                )
                for c in range(2)
            ],
            axis=0,
        ).astype(bf16)
        for j in range(touched):
            right = coef_ref[first : first + GROUP, j].reshape(GROUP * LANES, LANES)
            got = jnp.dot(left, right, preferred_element_type=f32)
            for c in range(2):
                terms[j, first : first + GROUP, c * LANES : (c + 1) * LANES] = got[c * GROUP : (c + 1) * GROUP]

    volume = out_ref.shape[0]
    rows = lax.broadcasted_iota(jnp.int32, (volume, blocks), 0)
    total = jnp.zeros(out_ref.shape, f32)
    for j in range(touched):
        onehot = jnp.where(rows == index_ref[pl.ds(j, 1), :], 1.0, 0.0).astype(bf16)
        whole = terms[j]
        for _ in range(3):
            piece = whole.astype(bf16)
            whole = whole - piece.astype(f32)
            total = total + jnp.dot(onehot, piece, preferred_element_type=f32)
    out_ref[...] = total


def volume_share(sums, model, index, coef, volume, scale):
    blocks, touched = coef.shape[:2]
    vmem = pl.BlockSpec(memory_space=pltpu.VMEM)
    return pl.pallas_call(
        functools.partial(volume_kernel, scale),
        in_specs=[vmem] * 4,
        out_specs=vmem,
        out_shape=jax.ShapeDtypeStruct((volume, 2 * LANES), f32),
        scratch_shapes=[
            pltpu.VMEM((2, blocks, LANES), f32),
            pltpu.VMEM((touched, blocks, 2 * LANES), f32),
        ],
        compiler_params=pltpu.CompilerParams(vmem_limit_bytes=24 * 2**20),
    )(sums, model, index, coef)


def shards(images, defocus, pose_bin, freq_sq, model_slice, interp_coef, block_index, volume):
    slabs = lax.axis_size("slab")
    shells = lax.axis_size("shell")
    kept, other, model, index, coef = weighted_sums(
        images, defocus, pose_bin, freq_sq, model_slice, interp_coef, block_index, slabs
    )
    other = lax.ppermute(other, "slab", [(i, i ^ 1) for i in range(slabs)])
    pair = (kept[: slabs // 2] + other.astype(f32)).astype(bf16)
    sums = lax.all_to_all(
        pair,
        "slab",
        split_axis=0,
        concat_axis=0,
        tiled=True,
        axis_index_groups=[list(range(side, slabs, 2)) for side in range(2)],
    )
    share = volume_share(sums, model, index, coef, volume, 1.0 / images.shape[0])
    owned = volume // (slabs * shells)
    shares = lax.all_to_all(share, ("slab", "shell"), split_axis=0, concat_axis=0, tiled=True)
    return jnp.sum(shares.reshape(slabs * shells, owned, 2, LANES), axis=0)


def solution(mesh):
    owned = 4
    volume = owned * mesh.shape["slab"] * mesh.shape["shell"]
    return jax.shard_map(
        functools.partial(shards, volume=volume),
        mesh=mesh,
        in_specs=(
            P("slab", None, "shell"),
            P("slab"),
            P("slab", None),
            P("shell"),
            P("slab", None, "shell"),
            P("slab", "shell", None, None, None),
            P("slab", "shell", None),
        ),
        out_specs=P(("slab", "shell"), None, None),
        check_vma=False,
    )
```

```python
import functools
import math

import jax
import jax.numpy as jnp
import numpy as np
from jax import lax
from jax.experimental import pallas as pl
from jax.experimental.pallas import tpu as pltpu
from jax.sharding import PartitionSpec as P

f32 = jnp.float32
bf16 = jnp.bfloat16
LANES = 128
GROUP = 8
WAYS = 1
LEAD = 2
AHEAD = 1
FINE = 64
COARSE = 32
ROUND = 12582912.0


def sine_coefficients():
    x = np.cos(np.pi * (np.arange(400) + 0.5) / 400)
    cheb = np.polynomial.chebyshev.Chebyshev.fit(x, np.sin(np.pi * x), 11, domain=[-1, 1])
    power = cheb.convert(kind=np.polynomial.Polynomial).coef
    return [float(power[2 * n + 1] * 2.0 ** (2 * n + 1)) for n in range(6)]


SINE = sine_coefficients()


def sine_of_turns(turns):
    r = turns - ((turns + ROUND) - ROUND)
    q = r * r
    s = q * SINE[5] + SINE[4]
    for n in (3, 2, 1, 0):
        s = s * q + SINE[n]
    return s * r


def fill_table(sines, cosines, turns):
    count = sines.shape[0]
    sines[0] = jnp.zeros_like(turns)
    cosines[0] = jnp.ones_like(turns)
    sines[1] = sine_of_turns(turns)
    cosines[1] = sine_of_turns(turns + 0.25)
    done = 2
    while done < count:
        last = done - 1
        s, c = sines[last], cosines[last]
        for n in range(1, min(done, count - last)):
            sines[last + n] = s * cosines[n] + c * sines[n]
            cosines[last + n] = c * cosines[n] - s * sines[n]
        done += min(done, count - last) - 1


def sums_kernel(
    half,
    unroll,
    piece,
    pose_hbm,
    images_hbm,
    defocus_hbm,
    freq_hbm,
    model_hbm,
    index_hbm,
    kept_ref,
    other_ref,
    model_out,
    index_out,
    pose,
    images,
    defocus,
    freq,
    steps,
    step_row,
    fine_sin,
    fine_cos,
    coarse_sin,
    coarse_cos,
    step_sem,
    small_sems,
    image_sems,
    late_sems,
    *acc,
):
    count = images.shape[0]
    blocks = freq.shape[0]
    small = [
        pltpu.make_async_copy(src, dst, small_sems.at[n])
        for n, (src, dst) in enumerate(((pose_hbm, pose), (defocus_hbm, defocus), (freq_hbm, freq)))
    ]
    for copy in small:
        copy.start()

    def image_copy(j):
        rows = pl.ds(j * piece, piece)
        return pltpu.make_async_copy(images_hbm.at[rows], images.at[rows], image_sems.at[j])

    lead = min(LEAD, count // piece)
    for j in range(lead):
        image_copy(j).start()
    late = [
        pltpu.make_async_copy(src, dst, late_sems.at[n])
        for n, (src, dst) in enumerate(
            ((model_hbm, model_out), (index_hbm, index_out))
        )
    ]

    for part in acc:
        part[...] = jnp.zeros_like(part)
    rows = lax.broadcasted_iota(jnp.int32, (2 * blocks, 2 * blocks), 0)
    cols = lax.broadcasted_iota(jnp.int32, (2 * blocks, 2 * blocks), 1)
    apart = jnp.where(cols == 2 * (rows % blocks) + rows // blocks, 1.0, 0.0).astype(bf16)
    for copy in small:
        copy.wait()
    for j in range(lead, count // piece):
        image_copy(j).start()
    for copy in late:
        copy.start()
    step_row[...] = (defocus[...].astype(f32) * 8.0).astype(jnp.int32)
    step_copy = pltpu.make_async_copy(step_row.at[0], steps, step_sem)
    step_copy.start()
    fill_table(fine_sin, fine_cos, freq[...] * (0.0625 / math.pi))
    fill_table(coarse_sin, coarse_cos, freq[...] * (4.0 / math.pi))
    step_copy.wait()
    side = lax.axis_index("slab") & 1

    def one(image):
        u, v = steps[image] >> 6, steps[image] & (FINE - 1)
        s = coarse_sin[u] * fine_cos[v] + coarse_cos[u] * fine_sin[v]
        both = jnp.dot(apart, images[image], preferred_element_type=f32)
        bin_ = pose[image]
        slot = ((bin_ & 1) ^ side) * half + (bin_ >> 1)
        return slot, s, both

    def body(j, _):
        for k in range(unroll // piece):
            image_copy(j * (unroll // piece) + k).wait()
        ready = []
        for k in range(unroll + AHEAD):
            if k < unroll:
                ready.append(one(unroll * j + k))
            if k >= AHEAD:
                slot, s, both = ready.pop(0)
                for part, value in enumerate((s * both[:blocks], s * both[blocks:], s * s)):
                    acc[3 * (k % WAYS) + part][slot] += value
        return 0

    lax.fori_loop(0, count // unroll, body, 0)
    for part in range(3):
        rows = slice(part * blocks, (part + 1) * blocks)
        whole = acc[part][...]
        for way in range(1, WAYS):
            whole = whole + acc[3 * way + part][...]
        kept_ref[:, rows] = whole[:half]
        other_ref[:, rows] = whole[half:].astype(other_ref.dtype)
    for copy in late:
        copy.wait()


def weighted_sums(images, defocus, pose_bin, freq_sq, model_slice, interp_coef, block_index, bins):
    count, _, width = images.shape
    blocks = width // LANES
    half = bins // 2
    unroll, piece = 16, 16
    rows = images.reshape(count, 2, blocks, LANES).transpose(0, 2, 1, 3).reshape(count, 2 * blocks, LANES)
    model = model_slice.reshape(2, blocks, LANES).transpose(1, 0, 2).reshape(2 * blocks, LANES)
    index = block_index[0].T
    hbm = pl.BlockSpec(memory_space=pltpu.HBM)
    vmem = pl.BlockSpec(memory_space=pltpu.VMEM)
    shapes = [
        ((half, 3 * blocks, LANES), f32),
        ((half, 3 * blocks, LANES), bf16),
        (model.shape, f32),
        (index.shape, jnp.int32),
    ]
    return pl.pallas_call(
        functools.partial(sums_kernel, half, unroll, piece),
        in_specs=[hbm] * 6,
        out_specs=[vmem] * 4,
        out_shape=[jax.ShapeDtypeStruct(shape, dtype) for shape, dtype in shapes],
        scratch_shapes=[
            pltpu.SMEM((count,), jnp.int32),
            pltpu.VMEM(rows.shape, bf16),
            pltpu.VMEM((1, count), bf16),
            pltpu.VMEM((blocks, LANES), f32),
            pltpu.SMEM((count,), jnp.int32),
            pltpu.VMEM((1, count), jnp.int32),
            pltpu.VMEM((FINE, blocks, LANES), f32),
            pltpu.VMEM((FINE, blocks, LANES), f32),
            pltpu.VMEM((COARSE, blocks, LANES), f32),
            pltpu.VMEM((COARSE, blocks, LANES), f32),
            pltpu.SemaphoreType.DMA,
            pltpu.SemaphoreType.DMA((3,)),
            pltpu.SemaphoreType.DMA((count // piece,)),
            pltpu.SemaphoreType.DMA((3,)),
        ]
        + [pltpu.VMEM((bins, blocks, LANES), f32)] * (3 * WAYS),
        cost_estimate=pl.CostEstimate(flops=20*10**9, bytes_accessed=16*10**6, transcendentals=0),
        compiler_params=pltpu.CompilerParams(vmem_limit_bytes=24 * 2**20),
    )(*[pltpu.with_memory_space_constraint(a, pltpu.HBM) for a in (pose_bin.reshape(-1), rows, defocus.reshape(1, -1), freq_sq.reshape(blocks, LANES), model, index)])


def volume_kernel(scale, sums_ref, model_ref, index_ref, coef_ref, out_ref, residual, terms):
    blocks, touched = coef_ref.shape[:2]
    total = sums_ref[0].astype(f32)
    for part in range(1, sums_ref.shape[0]):
        total = total + sums_ref[part].astype(f32)
    power = total[2 * blocks :]
    for c in range(2):
        model = model_ref[pl.ds(c, blocks, 2), :]
        residual[c] = (power * model - total[c * blocks : (c + 1) * blocks]) * scale

    row = lax.broadcasted_iota(jnp.int32, (GROUP, LANES), 0)
    for first in range(0, blocks, GROUP):
        left = jnp.concatenate(
            [
                jnp.concatenate(
                    [jnp.where(row == m, residual[c, first : first + GROUP], 0.0) for m in range(GROUP)],
                    axis=1,
                )
                for c in range(2)
            ],
            axis=0,
        ).astype(bf16)
        for j in range(touched):
            right = coef_ref[first : first + GROUP, j].reshape(GROUP * LANES, LANES)
            got = jnp.dot(left, right, preferred_element_type=f32)
            for c in range(2):
                terms[j, first : first + GROUP, c * LANES : (c + 1) * LANES] = got[c * GROUP : (c + 1) * GROUP]

    volume = out_ref.shape[0]
    rows = lax.broadcasted_iota(jnp.int32, (volume, blocks), 0)
    total = jnp.zeros(out_ref.shape, f32)
    for j in range(touched):
        onehot = jnp.where(rows == index_ref[pl.ds(j, 1), :], 1.0, 0.0).astype(bf16)
        whole = terms[j]
        for _ in range(3):
            piece = whole.astype(bf16)
            whole = whole - piece.astype(f32)
            total = total + jnp.dot(onehot, piece, preferred_element_type=f32)
    out_ref[...] = total


def volume_share(sums, model, index, coef, volume, scale):
    blocks, touched = coef.shape[:2]
    vmem = pl.BlockSpec(memory_space=pltpu.VMEM)
    return pl.pallas_call(
        functools.partial(volume_kernel, scale),
        in_specs=[vmem] * 4,
        out_specs=vmem,
        out_shape=jax.ShapeDtypeStruct((volume, 2 * LANES), f32),
        scratch_shapes=[
            pltpu.VMEM((2, blocks, LANES), f32),
            pltpu.VMEM((touched, blocks, 2 * LANES), f32),
        ],
        compiler_params=pltpu.CompilerParams(vmem_limit_bytes=24 * 2**20),
    )(sums, model, index, coef)


def shards(images, defocus, pose_bin, freq_sq, model_slice, interp_coef, block_index, volume):
    slabs = lax.axis_size("slab")
    shells = lax.axis_size("shell")
    kept, other, model, index = weighted_sums(
        images, defocus, pose_bin, freq_sq, model_slice, interp_coef, block_index, slabs
    )
    other = lax.ppermute(other, "slab", [(i, i ^ 1) for i in range(slabs)])
    pair = (kept + other.astype(f32)).astype(bf16)
    sums = lax.all_to_all(
        pair,
        "slab",
        split_axis=0,
        concat_axis=0,
        tiled=True,
        axis_index_groups=[list(range(side, slabs, 2)) for side in range(2)],
    )
    share = volume_share(sums, model, index, interp_coef[0], volume, 1.0 / images.shape[0])
    owned = volume // (slabs * shells)
    shares = lax.all_to_all(share, ("slab", "shell"), split_axis=0, concat_axis=0, tiled=True)
    return jnp.sum(shares.reshape(slabs * shells, owned, 2, LANES), axis=0)


def solution(mesh):
    owned = 4
    volume = owned * mesh.shape["slab"] * mesh.shape["shell"]
    return jax.shard_map(
        functools.partial(shards, volume=volume),
        mesh=mesh,
        in_specs=(
            P("slab", None, "shell"),
            P("slab"),
            P("slab", None),
            P("shell"),
            P("slab", None, "shell"),
            P("slab", "shell", None, None, None),
            P("slab", "shell", None),
        ),
        out_specs=P(("slab", "shell"), None, None),
        check_vma=False,
    )
```

```python
import functools
import math

import jax
import jax.numpy as jnp
import numpy as np
from jax import lax
from jax.experimental import pallas as pl
from jax.experimental.pallas import tpu as pltpu
from jax.sharding import PartitionSpec as P

f32 = jnp.float32
bf16 = jnp.bfloat16
LANES = 128
GROUP = 8
LEAD = 2
FINE = 64
COARSE = 32
COUNT_ROWS = 16
ROUND = 12582912.0


HBM = pl.BlockSpec(memory_space=pltpu.HBM)
VMEM = pl.BlockSpec(memory_space=pltpu.VMEM)


def sine_coefficients():
    x = np.cos(np.pi * (np.arange(400) + 0.5) / 400)
    cheb = np.polynomial.chebyshev.Chebyshev.fit(x, np.sin(np.pi * x), 11, domain=[-1, 1])
    power = cheb.convert(kind=np.polynomial.Polynomial).coef
    return [float(power[2 * n + 1] * 2.0 ** (2 * n + 1)) for n in range(6)]


SINE = sine_coefficients()


def sine_of_turns(turns):
    r = turns - ((turns + ROUND) - ROUND)
    q = r * r
    s = q * SINE[5] + SINE[4]
    for n in (3, 2, 1, 0):
        s = s * q + SINE[n]
    return s * r


def in_hbm(arrays):
    return [pltpu.with_memory_space_constraint(a, pltpu.HBM) for a in arrays]


def fill_table(sines, cosines, turns):
    count = sines.shape[0]
    sines[0] = jnp.zeros_like(turns)
    cosines[0] = jnp.ones_like(turns)
    sines[1] = sine_of_turns(turns)
    cosines[1] = sine_of_turns(turns + 0.25)
    done = 2
    while done < count:
        last = done - 1
        s, c = sines[last], cosines[last]
        for n in range(1, min(done, count - last)):
            sines[last + n] = s * cosines[n] + c * sines[n]
            cosines[last + n] = c * cosines[n] - s * sines[n]
        done += min(done, count - last) - 1


def sums_kernel(
    half,
    unroll,
    piece,
    pose_hbm,
    images_hbm,
    defocus_hbm,
    freq_hbm,
    kept_ref,
    other_ref,
    fine_sin,
    fine_cos,
    coarse_sin,
    coarse_cos,
    freq,
    pose,
    pose_row,
    images,
    defocus,
    steps,
    step_row,
    step_sem,
    small_sems,
    image_sems,
    counts,
    *acc,
):
    count = images.shape[0]
    blocks = freq.shape[0]
    small = [
        pltpu.make_async_copy(src, dst, small_sems.at[n])
        for n, (src, dst) in enumerate(((defocus_hbm, defocus), (freq_hbm, freq), (pose_hbm.at[0], pose), (pose_hbm, pose_row)))
    ]
    for copy in small:
        copy.start()

    def image_copy(j):
        rows = pl.ds(j * piece, piece)
        return pltpu.make_async_copy(images_hbm.at[rows], images.at[rows], image_sems.at[j])

    lead = min(LEAD, count // piece)
    for j in range(lead):
        image_copy(j).start()
    for part in acc:
        part[...] = jnp.zeros_like(part)
    rows = lax.broadcasted_iota(jnp.int32, (2 * blocks, 2 * blocks), 0)
    cols = lax.broadcasted_iota(jnp.int32, (2 * blocks, 2 * blocks), 1)
    apart = jnp.where(cols == 2 * (rows % blocks) + rows // blocks, 1.0, 0.0).astype(bf16)
    for copy in small:
        copy.wait()
    for j in range(lead, count // piece):
        image_copy(j).start()
    side = lax.axis_index("slab") & 1
    step_row[...] = (defocus[...].astype(f32) * 8.0).astype(jnp.int32)
    step_copy = pltpu.make_async_copy(step_row.at[0], steps, step_sem)
    step_copy.start()
    fill_table(fine_sin, fine_cos, freq[...] * (0.0625 / math.pi))
    fill_table(coarse_sin, coarse_cos, freq[...] * (4.0 / math.pi))
    rows = lax.broadcasted_iota(jnp.int32, (count, count), 0)
    cols = lax.broadcasted_iota(jnp.int32, (count, count), 1)
    diagonal = jnp.where(rows == cols, defocus[...].astype(f32), 0.0).astype(bf16)
    spread = jnp.dot(diagonal, jnp.ones((count, LANES), bf16), preferred_element_type=f32)
    eighths = (spread * 8.0).astype(jnp.int32)
    bins = 2 * half
    place = ((pose_row[...] & 1) ^ side) * half + (pose_row[...] >> 1)
    place = place * COUNT_ROWS + (step_row[...] >> 7)
    chosen = lax.broadcasted_iota(jnp.int32, (bins * COUNT_ROWS, count), 0) == place
    chosen = jnp.where(chosen, 1.0, 0.0).astype(bf16)
    named = (eighths & (LANES - 1)) == lax.broadcasted_iota(jnp.int32, (count, LANES), 1)
    named = jnp.where(named, 1.0, 0.0).astype(bf16)
    counts[...] = jnp.dot(chosen, named, preferred_element_type=f32)
    step_copy.wait()

    def one(image):
        u, v = steps[image] >> 6, steps[image] & (FINE - 1)
        s = coarse_sin[u] * fine_cos[v] + coarse_cos[u] * fine_sin[v]
        both = jnp.dot(apart, images[image], preferred_element_type=f32)
        bin_ = pose[image]
        slot = ((bin_ & 1) ^ side) * half + (bin_ >> 1)
        return slot, s, both

    def body(j, _):
        for k in range(unroll // piece):
            image_copy(j * (unroll // piece) + k).wait()
        for k in range(unroll):
            slot, s, both = one(unroll * j + k)
            for part, value in enumerate((s * both[:blocks], s * both[blocks:])):
                acc[part][slot] += value
        return 0

    lax.fori_loop(0, count // unroll, body, 0)
    numbers = counts[...].reshape(bins, COUNT_ROWS, LANES)
    for first, part in ((0, acc[0][...]), (blocks, acc[1][...]), (2 * blocks, numbers)):
        rows = slice(first, first + part.shape[1])
        kept_ref[:, rows] = part[:half]
        other_ref[:, rows] = part[half:].astype(other_ref.dtype)


def weighted_sums(images, defocus, pose_bin, freq_sq, bins):
    count, _, width = images.shape
    blocks = width // LANES
    half = bins // 2
    unroll, piece = 32, 16
    rows = images.reshape(count, 2, blocks, LANES).transpose(0, 2, 1, 3).reshape(count, 2 * blocks, LANES)
    height = 2 * blocks + COUNT_ROWS
    return pl.pallas_call(
        functools.partial(sums_kernel, half, unroll, piece),
        in_specs=[HBM] * 4,
        out_specs=[VMEM] * 7,
        out_shape=[
            jax.ShapeDtypeStruct((half, height, LANES), f32),
            jax.ShapeDtypeStruct((half, height, LANES), bf16),
        ]
        + [jax.ShapeDtypeStruct((n, blocks, LANES), f32) for n in (FINE, FINE, COARSE, COARSE)]
        + [jax.ShapeDtypeStruct((blocks, LANES), f32)],
        scratch_shapes=[
            pltpu.SMEM((count,), jnp.int32),
            pltpu.VMEM((1, count), jnp.int32),
            pltpu.VMEM(rows.shape, bf16),
            pltpu.VMEM((1, count), bf16),
            pltpu.SMEM((count,), jnp.int32),
            pltpu.VMEM((1, count), jnp.int32),
            pltpu.SemaphoreType.DMA,
            pltpu.SemaphoreType.DMA((4,)),
            pltpu.SemaphoreType.DMA((count // piece,)),
            pltpu.VMEM((bins * COUNT_ROWS, LANES), f32),
            pltpu.VMEM((bins, blocks, LANES), f32),
            pltpu.VMEM((bins, blocks, LANES), f32),
        ],
        cost_estimate=pl.CostEstimate(flops=20 * 10**9, bytes_accessed=16 * 10**6, transcendentals=0),
        compiler_params=pltpu.CompilerParams(vmem_limit_bytes=24 * 2**20),
    )(*in_hbm([pose_bin.reshape(1, -1), rows, defocus.reshape(1, -1), freq_sq.reshape(blocks, LANES)]))


def turn_by(cosine, sine, by):
    return cosine * by[0] - sine * by[1], sine * by[0] + cosine * by[1]


def tables_kernel(
    model_hbm, index_hbm, fine_sin, fine_cos, coarse_sin, coarse_cos, freq, model, index, fine, coarse, sems
):
    blocks = index.shape[1]
    copies = [
        pltpu.make_async_copy(src, dst, sems.at[n])
        for n, (src, dst) in enumerate(((model_hbm, model), (index_hbm, index)))
    ]
    for copy in copies:
        copy.start()

    first = lax.broadcasted_iota(jnp.int32, (8, LANES), 0).astype(f32)

    def entry(cosines, sines, k, n):
        rows = pl.ds(n * blocks + k, 1)
        return cosines[rows, :], sines[rows, :]

    def one(k):
        lanes = [pl.ds(pl.multiple_of((2 * k + part) * LANES, LANES), LANES) for part in range(2)]
        f = freq[pl.ds(k, 1), :]
        angle = first * (f * (0.125 / math.pi))
        pair = [(sine_of_turns(angle + 0.25), sine_of_turns(angle))]
        by = entry(fine_cos, fine_sin, k, 16)
        for _ in range(FINE // 8 - 1):
            pair.append(turn_by(*pair[-1], by))
        for part in range(2):
            fine[:, lanes[part]] = jnp.concatenate([p[part] for p in pair], axis=0).astype(bf16)
        angle = first * (f * (16.0 / math.pi))
        angle = angle - ((angle + ROUND) - ROUND)
        even = (sine_of_turns(angle + 0.25), sine_of_turns(angle))
        by = entry(coarse_cos, coarse_sin, k, 16)
        pair = [even, turn_by(*even, turn_by(*by, by))]
        by = entry(coarse_cos, coarse_sin, k, 2)
        pair += [turn_by(*p, by) for p in pair]
        coarse[:, lanes[0]] = jnp.concatenate([p[0] for p in pair], axis=0)
        coarse[:, lanes[1]] = jnp.concatenate([-p[1] for p in pair], axis=0)

    def body(j, _):
        for k in range(GROUP):
            one(GROUP * j + k)
        return 0

    lax.fori_loop(0, blocks // GROUP, body, 0)
    for copy in copies:
        copy.wait()


def tables(angles, model_slice, block_index):
    blocks = block_index.shape[1]
    model = model_slice.reshape(2, blocks, LANES).transpose(1, 0, 2).reshape(2 * blocks, LANES)
    index = block_index[0].T
    shapes = [
        (model.shape, f32),
        (index.shape, jnp.int32),
        ((FINE, 2 * blocks * LANES), bf16),
        ((COARSE, 2 * blocks * LANES), f32),
    ]
    return pl.pallas_call(
        tables_kernel,
        in_specs=[HBM] * 2 + [VMEM] * 5,
        out_specs=[VMEM] * 4,
        out_shape=[jax.ShapeDtypeStruct(shape, dtype) for shape, dtype in shapes],
        scratch_shapes=[
            pltpu.SemaphoreType.DMA((2,)),
        ],
        cost_estimate=pl.CostEstimate(flops=10**9, bytes_accessed=10**6, transcendentals=0),
        compiler_params=pltpu.CompilerParams(vmem_limit_bytes=8 * 2**20),
    )(*in_hbm([model, index]), *[a.reshape(-1, LANES) for a in angles])


def volume_kernel(
    scale, sums_ref, model_ref, index_ref, fine, coarse, coef_ref, out_ref, power, residual, terms
):
    blocks, touched = coef_ref.shape[:2]
    total = sums_ref[0].astype(f32)
    for part in range(1, sums_ref.shape[0]):
        total = total + sums_ref[part].astype(f32)
    counts = total[2 * blocks :]
    counts = jnp.concatenate([counts, pltpu.roll(counts, FINE, 1)], axis=0)[:, :FINE]
    named = jnp.sum(counts)
    high = counts.astype(bf16)
    counts = jnp.concatenate([high, (counts - high.astype(f32)).astype(bf16)], axis=0)
    for first in range(0, blocks, GROUP):
        lanes = slice(2 * first * LANES, 2 * (first + GROUP) * LANES)
        inner = jnp.dot(counts, fine[:, lanes], preferred_element_type=f32)
        cosine = (inner[:COARSE] + inner[COARSE:]) * coarse[:, lanes]
        cosine = sum(cosine[n : n + 8] for n in range(0, COARSE, 8))
        for k in range(GROUP):
            both = cosine[:, 2 * k * LANES : (2 * k + 1) * LANES] + cosine[:, (2 * k + 1) * LANES : (2 * k + 2) * LANES]
            both = jnp.sum(both, axis=0, keepdims=True)
            power[first + k : first + k + 1, :] = (named - both) * 0.5

    for c in range(2):
        model = model_ref[pl.ds(c, blocks, 2), :]
        residual[c] = (power[...] * model - total[c * blocks : (c + 1) * blocks]) * scale

    row = lax.broadcasted_iota(jnp.int32, (GROUP, LANES), 0)
    for first in range(0, blocks, GROUP):
        left = jnp.concatenate(
            [
                jnp.concatenate(
                    [jnp.where(row == m, residual[c, first : first + GROUP], 0.0) for m in range(GROUP)],
                    axis=1,
                )
                for c in range(2)
            ],
            axis=0,
        ).astype(bf16)
        for j in range(touched):
            right = coef_ref[first : first + GROUP, j].reshape(GROUP * LANES, LANES)
            got = jnp.dot(left, right, preferred_element_type=f32)
            for c in range(2):
                terms[j, first : first + GROUP, c * LANES : (c + 1) * LANES] = got[c * GROUP : (c + 1) * GROUP]

    volume = out_ref.shape[0]
    rows = lax.broadcasted_iota(jnp.int32, (volume, blocks), 0)
    total = jnp.zeros(out_ref.shape, f32)
    for j in range(touched):
        onehot = jnp.where(rows == index_ref[pl.ds(j, 1), :], 1.0, 0.0).astype(bf16)
        whole = terms[j]
        for _ in range(3):
            piece = whole.astype(bf16)
            whole = whole - piece.astype(f32)
            total = total + jnp.dot(onehot, piece, preferred_element_type=f32)
    out_ref[...] = total


def volume_share(sums, loaded, coef, volume, scale):
    blocks, touched = coef.shape[:2]
    return pl.pallas_call(
        functools.partial(volume_kernel, scale),
        in_specs=[VMEM] * 6,
        out_specs=VMEM,
        out_shape=jax.ShapeDtypeStruct((volume, 2 * LANES), f32),
        scratch_shapes=[
            pltpu.VMEM((blocks, LANES), f32),
            pltpu.VMEM((2, blocks, LANES), f32),
            pltpu.VMEM((touched, blocks, 2 * LANES), f32),
        ],
        compiler_params=pltpu.CompilerParams(vmem_limit_bytes=16 * 2**20),
    )(sums, *loaded, coef)


def shards(images, defocus, pose_bin, freq_sq, model_slice, interp_coef, block_index, volume):
    slabs = lax.axis_size("slab")
    shells = lax.axis_size("shell")
    kept, other, *angles = weighted_sums(images, defocus, pose_bin, freq_sq, slabs)
    loaded = tables(angles, model_slice, block_index)
    other = lax.ppermute(other, "slab", [(i, i ^ 1) for i in range(slabs)])
    pair = (kept + other.astype(f32)).astype(bf16)
    pair, loaded = lax.optimization_barrier((pair, loaded))
    sums = lax.all_to_all(
        pair,
        "slab",
        split_axis=0,
        concat_axis=0,
        tiled=True,
        axis_index_groups=[list(range(side, slabs, 2)) for side in range(2)],
    )
    share = volume_share(sums, loaded, interp_coef[0], volume, 1.0 / images.shape[0])
    owned = volume // (slabs * shells)
    shares = lax.all_to_all(share, ("slab", "shell"), split_axis=0, concat_axis=0, tiled=True)
    return jnp.sum(shares.reshape(slabs * shells, owned, 2, LANES), axis=0)


def solution(mesh):
    owned = 4
    volume = owned * mesh.shape["slab"] * mesh.shape["shell"]
    return jax.shard_map(
        functools.partial(shards, volume=volume),
        mesh=mesh,
        in_specs=(
            P("slab", None, "shell"),
            P("slab"),
            P("slab", None),
            P("shell"),
            P("slab", None, "shell"),
            P("slab", "shell", None, None, None),
            P("slab", "shell", None),
        ),
        out_specs=P(("slab", "shell"), None, None),
        check_vma=False,
    )
```

```python
import functools
import math

import jax
import jax.numpy as jnp
import numpy as np
from jax import lax
from jax.experimental import pallas as pl
from jax.experimental.pallas import tpu as pltpu
from jax.sharding import PartitionSpec as P

f32 = jnp.float32
bf16 = jnp.bfloat16
LANES = 128
GROUP = 8
LEAD = 2
FINE = 64
COARSE = 32
COARSE_USED = 26
COUNT_ROWS = 16
ROUND = 12582912.0


HBM = pl.BlockSpec(memory_space=pltpu.HBM)
VMEM = pl.BlockSpec(memory_space=pltpu.VMEM)


def sine_coefficients():
    x = np.cos(np.pi * (np.arange(400) + 0.5) / 400)
    cheb = np.polynomial.chebyshev.Chebyshev.fit(x, np.sin(np.pi * x), 11, domain=[-1, 1])
    power = cheb.convert(kind=np.polynomial.Polynomial).coef
    return [float(power[2 * n + 1] * 2.0 ** (2 * n + 1)) for n in range(6)]


SINE = sine_coefficients()


def cosine_coefficients():
    x = np.cos(np.pi * (np.arange(400) + 0.5) / 400)
    cheb = np.polynomial.chebyshev.Chebyshev.fit(x, np.cos(np.pi * x), 12, domain=[-1, 1])
    power = cheb.convert(kind=np.polynomial.Polynomial).coef
    return [float(power[2 * n] * 4.0**n) for n in range(7)]


COSINE = cosine_coefficients()


def horner(coefficients, q):
    value = q * coefficients[-1] + coefficients[-2]
    for c in coefficients[-3::-1]:
        value = value * q + c
    return value


def cosine_and_sine(r):
    q = r * r
    return horner(COSINE, q), horner(SINE, q) * r


def sine_of_turns(turns):
    r = turns - ((turns + ROUND) - ROUND)
    q = r * r
    s = q * SINE[5] + SINE[4]
    for n in (3, 2, 1, 0):
        s = s * q + SINE[n]
    return s * r


def in_hbm(arrays):
    return [pltpu.with_memory_space_constraint(a, pltpu.HBM) for a in arrays]


def fill_table(sines, cosines, turns):
    count = sines.shape[0]
    sines[0] = jnp.zeros_like(turns)
    cosines[0] = jnp.ones_like(turns)
    sines[1] = sine_of_turns(turns)
    cosines[1] = sine_of_turns(turns + 0.25)
    done = 2
    while done < count:
        last = done - 1
        s, c = sines[last], cosines[last]
        for n in range(1, min(done, count - last)):
            sines[last + n] = s * cosines[n] + c * sines[n]
            cosines[last + n] = c * cosines[n] - s * sines[n]
        done += min(done, count - last) - 1


def sums_kernel(
    half,
    unroll,
    piece,
    pose_hbm,
    images_hbm,
    defocus_hbm,
    freq_hbm,
    model_hbm,
    index_hbm,
    kept_ref,
    other_ref,
    fine_sin,
    fine_cos,
    coarse_sin,
    coarse_cos,
    freq,
    model,
    index,
    pose,
    pose_row,
    images,
    defocus,
    steps,
    step_row,
    step_sem,
    small_sems,
    image_sems,
    late_sems,
):
    count = images.shape[0]
    blocks = freq.shape[0]
    small = [
        pltpu.make_async_copy(src, dst, small_sems.at[n])
        for n, (src, dst) in enumerate(
            ((defocus_hbm, defocus), (freq_hbm, freq), (pose_hbm.at[0], pose), (pose_hbm, pose_row))
        )
    ]
    for copy in small:
        copy.start()

    def image_copy(j):
        rows = pl.ds(j * piece, piece)
        return pltpu.make_async_copy(images_hbm.at[rows], images.at[rows], image_sems.at[j])

    lead = min(LEAD, count // piece)
    for j in range(lead):
        image_copy(j).start()
    kept_ref[...] = jnp.zeros_like(kept_ref)
    rows = lax.broadcasted_iota(jnp.int32, (2 * blocks, 2 * blocks), 0)
    cols = lax.broadcasted_iota(jnp.int32, (2 * blocks, 2 * blocks), 1)
    apart = jnp.where(cols == 2 * (rows % blocks) + rows // blocks, 1.0, 0.0).astype(bf16)
    for copy in small:
        copy.wait()
    for j in range(lead, count // piece):
        image_copy(j).start()
    late = [
        pltpu.make_async_copy(src, dst, late_sems.at[n])
        for n, (src, dst) in enumerate(((model_hbm, model), (index_hbm, index)))
    ]
    for copy in late:
        copy.start()
    side = lax.axis_index("slab") & 1
    step_row[...] = (defocus[...].astype(f32) * 8.0).astype(jnp.int32)
    step_copy = pltpu.make_async_copy(step_row.at[0], steps, step_sem)
    step_copy.start()
    fill_table(fine_sin, fine_cos, freq[...] * (0.0625 / math.pi))
    fill_table(coarse_sin, coarse_cos, freq[...] * (4.0 / math.pi))
    rows = lax.broadcasted_iota(jnp.int32, (count, count), 0)
    cols = lax.broadcasted_iota(jnp.int32, (count, count), 1)
    diagonal = jnp.where(rows == cols, defocus[...].astype(f32), 0.0).astype(bf16)
    spread = jnp.dot(diagonal, jnp.ones((count, LANES), bf16), preferred_element_type=f32)
    eighths = (spread * 8.0).astype(jnp.int32)
    bins = 2 * half
    place = ((pose_row[...] & 1) ^ side) * half + (pose_row[...] >> 1)
    place = place * COUNT_ROWS + (step_row[...] >> 7)
    chosen = lax.broadcasted_iota(jnp.int32, (bins * COUNT_ROWS, count), 0) == place
    chosen = jnp.where(chosen, 1.0, 0.0).astype(bf16)
    named = (eighths & (LANES - 1)) == lax.broadcasted_iota(jnp.int32, (count, LANES), 1)
    named = jnp.where(named, 1.0, 0.0).astype(bf16)
    numbers = jnp.dot(chosen, named, preferred_element_type=f32)
    kept_ref[:, 2 * blocks :] = numbers.reshape(bins, COUNT_ROWS, LANES)
    step_copy.wait()

    def one(image):
        u, v = steps[image] >> 6, steps[image] & (FINE - 1)
        s = coarse_sin[u] * fine_cos[v] + coarse_cos[u] * fine_sin[v]
        both = jnp.dot(apart, images[image], preferred_element_type=f32)
        bin_ = pose[image]
        slot = ((bin_ & 1) ^ side) * half + (bin_ >> 1)
        return slot, s, both

    def body(j, _):
        for k in range(unroll // piece):
            image_copy(j * (unroll // piece) + k).wait()
        for k in range(unroll):
            slot, s, both = one(unroll * j + k)
            for part, value in enumerate((s * both[:blocks], s * both[blocks:])):
                kept_ref[slot, part * blocks : (part + 1) * blocks] += value
        return 0

    lax.fori_loop(0, count // unroll, body, 0)
    other_ref[...] = kept_ref[half:].astype(other_ref.dtype)
    for copy in late:
        copy.wait()


def weighted_sums(images, defocus, pose_bin, freq_sq, model_slice, block_index, bins):
    count, _, width = images.shape
    blocks = width // LANES
    half = bins // 2
    unroll, piece = 32, 16
    rows = images.reshape(count, 2, blocks, LANES).transpose(0, 2, 1, 3).reshape(count, 2 * blocks, LANES)
    height = 2 * blocks + COUNT_ROWS
    model = model_slice.reshape(2, blocks, LANES).transpose(1, 0, 2).reshape(2 * blocks, LANES)
    index = block_index[0].T
    return pl.pallas_call(
        functools.partial(sums_kernel, half, unroll, piece),
        in_specs=[HBM] * 6,
        out_specs=[VMEM] * 9,
        out_shape=[
            jax.ShapeDtypeStruct((bins, height, LANES), f32),
            jax.ShapeDtypeStruct((half, height, LANES), bf16),
        ]
        + [jax.ShapeDtypeStruct((n, blocks, LANES), f32) for n in (FINE, FINE, COARSE_USED, COARSE_USED)]
        + [
            jax.ShapeDtypeStruct((blocks, LANES), f32),
            jax.ShapeDtypeStruct(model.shape, f32),
            jax.ShapeDtypeStruct(index.shape, jnp.int32),
        ],
        scratch_shapes=[
            pltpu.SMEM((count,), jnp.int32),
            pltpu.VMEM((1, count), jnp.int32),
            pltpu.VMEM(rows.shape, bf16),
            pltpu.VMEM((1, count), bf16),
            pltpu.SMEM((count,), jnp.int32),
            pltpu.VMEM((1, count), jnp.int32),
            pltpu.SemaphoreType.DMA,
            pltpu.SemaphoreType.DMA((4,)),
            pltpu.SemaphoreType.DMA((count // piece,)),
            pltpu.SemaphoreType.DMA((2,)),
        ],
        compiler_params=pltpu.CompilerParams(vmem_limit_bytes=24 * 2**20),
    )(
        *in_hbm(
            [
                pose_bin.reshape(1, -1),
                rows,
                defocus.reshape(1, -1),
                freq_sq.reshape(blocks, LANES),
                model,
                index,
            ]
        )
    )


def turn_by(cosine, sine, by):
    return cosine * by[0] - sine * by[1], sine * by[0] + cosine * by[1]


def tables_kernel(fine_sin, fine_cos, coarse_sin, coarse_cos, freq, fine, coarse):
    blocks = freq.shape[0]
    first = lax.broadcasted_iota(jnp.int32, (8, LANES), 0).astype(f32)

    def entry(cosines, sines, k, n):
        rows = pl.ds(n * blocks + k, 1)
        return cosines[rows, :], sines[rows, :]

    def one(k):
        lanes = [pl.ds(pl.multiple_of((2 * k + part) * LANES, LANES), LANES) for part in range(2)]
        f = freq[pl.ds(k, 1), :]
        angle = first * (f * (0.125 / math.pi))
        pair = [cosine_and_sine(angle)]
        by = entry(fine_cos, fine_sin, k, 16)
        for _ in range(FINE // 8 - 1):
            pair.append(turn_by(*pair[-1], by))
        for part in range(2):
            fine[:, lanes[part]] = jnp.concatenate([p[part] for p in pair], axis=0).astype(bf16)
        angle = first * (f * (16.0 / math.pi))
        angle = angle - ((angle + ROUND) - ROUND)
        even = cosine_and_sine(angle)
        by = entry(coarse_cos, coarse_sin, k, 16)
        pair = [even, turn_by(*even, turn_by(*by, by))]
        by = entry(coarse_cos, coarse_sin, k, 2)
        pair += [turn_by(*p, by) for p in pair]
        coarse[:, lanes[0]] = jnp.concatenate([p[0] for p in pair], axis=0)
        coarse[:, lanes[1]] = jnp.concatenate([-p[1] for p in pair], axis=0)

    def body(j, _):
        for k in range(GROUP):
            one(GROUP * j + k)
        return 0

    lax.fori_loop(0, blocks // GROUP, body, 0)


def tables(angles):
    blocks = angles[-1].shape[0]
    shapes = [((FINE, 2 * blocks * LANES), bf16), ((COARSE, 2 * blocks * LANES), f32)]
    return pl.pallas_call(
        tables_kernel,
        in_specs=[VMEM] * 5,
        out_specs=[VMEM] * 2,
        out_shape=[jax.ShapeDtypeStruct(shape, dtype) for shape, dtype in shapes],
        cost_estimate=pl.CostEstimate(flops=20 * 10**9, bytes_accessed=16 * 10**6, transcendentals=0),
        compiler_params=pltpu.CompilerParams(vmem_limit_bytes=8 * 2**20),
    )(*[a.reshape(-1, LANES) for a in angles])


def volume_kernel(
    scale, sums_ref, model_ref, index_ref, fine, coarse, coef_ref, out_ref, power, residual, terms
):
    blocks, touched = coef_ref.shape[:2]
    total = sums_ref[0].astype(f32)
    for part in range(1, sums_ref.shape[0]):
        total = total + sums_ref[part].astype(f32)
    counts = total[2 * blocks :]
    counts = jnp.concatenate([counts, pltpu.roll(counts, FINE, 1)], axis=0)[:, :FINE]
    named = jnp.sum(counts)
    high = counts.astype(bf16)
    counts = jnp.concatenate([high, (counts - high.astype(f32)).astype(bf16)], axis=0)
    for first in range(0, blocks, GROUP):
        lanes = slice(2 * first * LANES, 2 * (first + GROUP) * LANES)
        inner = jnp.dot(counts, fine[:, lanes], preferred_element_type=f32)
        cosine = (inner[:COARSE] + inner[COARSE:]) * coarse[:, lanes]
        cosine = sum(cosine[n : n + 8] for n in range(0, COARSE, 8))
        for k in range(GROUP):
            both = cosine[:, 2 * k * LANES : (2 * k + 1) * LANES] + cosine[:, (2 * k + 1) * LANES : (2 * k + 2) * LANES]
            both = jnp.sum(both, axis=0, keepdims=True)
            power[first + k : first + k + 1, :] = (named - both) * 0.5

    for c in range(2):
        model = model_ref[pl.ds(c, blocks, 2), :]
        residual[c] = (power[...] * model - total[c * blocks : (c + 1) * blocks]) * scale

    row = lax.broadcasted_iota(jnp.int32, (GROUP, LANES), 0)
    for first in range(0, blocks, GROUP):
        left = jnp.concatenate(
            [
                jnp.concatenate(
                    [jnp.where(row == m, residual[c, first : first + GROUP], 0.0) for m in range(GROUP)],
                    axis=1,
                )
                for c in range(2)
            ],
            axis=0,
        ).astype(bf16)
        for j in range(touched):
            right = coef_ref[first : first + GROUP, j].reshape(GROUP * LANES, LANES)
            got = jnp.dot(left, right, preferred_element_type=f32)
            for c in range(2):
                terms[j, first : first + GROUP, c * LANES : (c + 1) * LANES] = got[c * GROUP : (c + 1) * GROUP]

    volume = out_ref.shape[0]
    rows = lax.broadcasted_iota(jnp.int32, (volume, blocks), 0)
    total = jnp.zeros(out_ref.shape, f32)
    for j in range(touched):
        onehot = jnp.where(rows == index_ref[pl.ds(j, 1), :], 1.0, 0.0).astype(bf16)
        whole = terms[j]
        for _ in range(2):
            piece = whole.astype(bf16)
            whole = whole - piece.astype(f32)
            total = total + jnp.dot(onehot, piece, preferred_element_type=f32)
    out_ref[...] = total


def volume_share(sums, loaded, coef, volume, scale):
    blocks, touched = coef.shape[:2]
    return pl.pallas_call(
        functools.partial(volume_kernel, scale),
        in_specs=[VMEM] * 6,
        out_specs=VMEM,
        out_shape=jax.ShapeDtypeStruct((volume, 2 * LANES), f32),
        scratch_shapes=[
            pltpu.VMEM((blocks, LANES), f32),
            pltpu.VMEM((2, blocks, LANES), f32),
            pltpu.VMEM((touched, blocks, 2 * LANES), f32),
        ],
        compiler_params=pltpu.CompilerParams(vmem_limit_bytes=16 * 2**20),
    )(sums, *loaded, coef)


def shards(images, defocus, pose_bin, freq_sq, model_slice, interp_coef, block_index, volume):
    slabs = lax.axis_size("slab")
    shells = lax.axis_size("shell")
    kept, other, *angles, model, index = weighted_sums(
        images, defocus, pose_bin, freq_sq, model_slice, block_index, slabs
    )
    loaded = [model, index, *tables(angles)]
    other = lax.ppermute(other, "slab", [(i, i ^ 1) for i in range(slabs)])
    half = slabs // 2
    pair = (kept[:half] + other.astype(f32)).astype(bf16)
    pair, loaded = lax.optimization_barrier((pair, loaded))
    sums = lax.all_to_all(
        pair,
        "slab",
        split_axis=0,
        concat_axis=0,
        tiled=True,
        axis_index_groups=[list(range(side, slabs, 2)) for side in range(2)],
    )
    share = volume_share(sums, loaded, interp_coef[0], volume, 1.0 / images.shape[0])
    owned = volume // (slabs * shells)
    shares = lax.all_to_all(share, ("slab", "shell"), split_axis=0, concat_axis=0, tiled=True)
    return jnp.sum(shares.reshape(slabs * shells, owned, 2, LANES), axis=0)


def solution(mesh):
    owned = 4
    volume = owned * mesh.shape["slab"] * mesh.shape["shell"]
    return jax.shard_map(
        functools.partial(shards, volume=volume),
        mesh=mesh,
        in_specs=(
            P("slab", None, "shell"),
            P("slab"),
            P("slab", None),
            P("shell"),
            P("slab", None, "shell"),
            P("slab", "shell", None, None, None),
            P("slab", "shell", None),
        ),
        out_specs=P(("slab", "shell"), None, None),
        check_vma=False,
    )
```

```python
import functools
import math

import jax
import jax.numpy as jnp
import numpy as np
from jax import lax
from jax.experimental import pallas as pl
from jax.experimental.pallas import tpu as pltpu
from jax.sharding import PartitionSpec as P

f32 = jnp.float32
bf16 = jnp.bfloat16
LANES = 128
GROUP = 8
LEAD = 2
FINE = 64
COARSE = 32
COARSE_USED = 26
COUNT_ROWS = 16
ROUND = 12582912.0


HBM = pl.BlockSpec(memory_space=pltpu.HBM)
VMEM = pl.BlockSpec(memory_space=pltpu.VMEM)


def sine_coefficients():
    x = np.cos(np.pi * (np.arange(400) + 0.5) / 400)
    cheb = np.polynomial.chebyshev.Chebyshev.fit(x, np.sin(np.pi * x), 11, domain=[-1, 1])
    power = cheb.convert(kind=np.polynomial.Polynomial).coef
    return [float(power[2 * n + 1] * 2.0 ** (2 * n + 1)) for n in range(6)]


SINE = sine_coefficients()


def cosine_coefficients():
    x = np.cos(np.pi * (np.arange(400) + 0.5) / 400)
    cheb = np.polynomial.chebyshev.Chebyshev.fit(x, np.cos(np.pi * x), 12, domain=[-1, 1])
    power = cheb.convert(kind=np.polynomial.Polynomial).coef
    return [float(power[2 * n] * 4.0**n) for n in range(7)]


COSINE = cosine_coefficients()


def horner(coefficients, q):
    value = q * coefficients[-1] + coefficients[-2]
    for c in coefficients[-3::-1]:
        value = value * q + c
    return value


def cosine_and_sine(r):
    q = r * r
    return horner(COSINE, q), horner(SINE, q) * r


def sine_of_turns(turns):
    r = turns - ((turns + ROUND) - ROUND)
    q = r * r
    s = q * SINE[5] + SINE[4]
    for n in (3, 2, 1, 0):
        s = s * q + SINE[n]
    return s * r


def in_hbm(arrays):
    return [pltpu.with_memory_space_constraint(a, pltpu.HBM) for a in arrays]


def fill_table(sines, cosines, turns):
    count = sines.shape[0]
    sines[0] = jnp.zeros_like(turns)
    cosines[0] = jnp.ones_like(turns)
    sines[1] = sine_of_turns(turns)
    cosines[1] = sine_of_turns(turns + 0.25)
    done = 2
    while done < count:
        last = done - 1
        s, c = sines[last], cosines[last]
        for n in range(1, min(done, count - last)):
            sines[last + n] = s * cosines[n] + c * sines[n]
            cosines[last + n] = c * cosines[n] - s * sines[n]
        done += min(done, count - last) - 1


def sums_kernel(
    half,
    unroll,
    piece,
    pose_hbm,
    images_hbm,
    defocus_hbm,
    freq_hbm,
    model_hbm,
    index_hbm,
    kept_ref,
    other_ref,
    fine_sin,
    fine_cos,
    coarse_sin,
    coarse_cos,
    freq,
    model,
    index,
    pose,
    pose_row,
    images,
    defocus,
    steps,
    step_row,
    step_sem,
    small_sems,
    image_sems,
    late_sems,
):
    count = images.shape[0]
    blocks = freq.shape[0]
    small = [
        pltpu.make_async_copy(src, dst, small_sems.at[n])
        for n, (src, dst) in enumerate(
            ((defocus_hbm, defocus), (freq_hbm, freq), (pose_hbm.at[0], pose), (pose_hbm, pose_row))
        )
    ]
    for copy in small:
        copy.start()

    def image_copy(j):
        rows = pl.ds(j * piece, piece)
        return pltpu.make_async_copy(images_hbm.at[rows], images.at[rows], image_sems.at[j])

    lead = min(LEAD, count // piece)
    for j in range(lead):
        image_copy(j).start()
    kept_ref[...] = jnp.zeros_like(kept_ref)
    rows = lax.broadcasted_iota(jnp.int32, (2 * blocks, 2 * blocks), 0)
    cols = lax.broadcasted_iota(jnp.int32, (2 * blocks, 2 * blocks), 1)
    apart = jnp.where(cols == 2 * (rows % blocks) + rows // blocks, 1.0, 0.0).astype(bf16)
    for copy in small:
        copy.wait()
    for j in range(lead, count // piece):
        image_copy(j).start()
    late = [
        pltpu.make_async_copy(src, dst, late_sems.at[n])
        for n, (src, dst) in enumerate(((model_hbm, model), (index_hbm, index)))
    ]
    for copy in late:
        copy.start()
    side = lax.axis_index("slab") & 1
    step_row[...] = (defocus[...].astype(f32) * 8.0).astype(jnp.int32)
    step_copy = pltpu.make_async_copy(step_row.at[0], steps, step_sem)
    step_copy.start()
    fill_table(fine_sin, fine_cos, freq[...] * (0.0625 / math.pi))
    fill_table(coarse_sin, coarse_cos, freq[...] * (4.0 / math.pi))
    bins = 2 * half
    place = ((pose_row[...] & 1) ^ side) * half + (pose_row[...] >> 1)
    place = place * COUNT_ROWS + (step_row[...] >> 7)
    chosen = lax.broadcasted_iota(jnp.int32, (bins * COUNT_ROWS, count), 0) == place
    chosen = jnp.where(chosen, 1.0, 0.0).astype(bf16)
    named = lax.broadcasted_iota(jnp.int32, (LANES, count), 0) == (step_row[...] & (LANES - 1))
    named = jnp.where(named, 1.0, 0.0).astype(bf16)
    numbers = lax.dot_general(chosen, named, (((1,), (1,)), ((), ())), preferred_element_type=f32)
    kept_ref[:, 2 * blocks :] = numbers.reshape(bins, COUNT_ROWS, LANES)
    step_copy.wait()

    def one(image):
        u, v = steps[image] >> 6, steps[image] & (FINE - 1)
        s = coarse_sin[u] * fine_cos[v] + coarse_cos[u] * fine_sin[v]
        both = jnp.dot(apart, images[image], preferred_element_type=f32)
        bin_ = pose[image]
        slot = ((bin_ & 1) ^ side) * half + (bin_ >> 1)
        return slot, s, both

    def body(j, _):
        for k in range(unroll // piece):
            image_copy(j * (unroll // piece) + k).wait()
        for k in range(unroll):
            slot, s, both = one(unroll * j + k)
            for part, value in enumerate((s * both[:blocks], s * both[blocks:])):
                kept_ref[slot, part * blocks : (part + 1) * blocks] += value
        return 0

    lax.fori_loop(0, count // unroll, body, 0)
    other_ref[...] = kept_ref[half:].astype(other_ref.dtype)
    for copy in late:
        copy.wait()


def weighted_sums(images, defocus, pose_bin, freq_sq, model_slice, block_index, bins):
    count, _, width = images.shape
    blocks = width // LANES
    half = bins // 2
    unroll, piece = 32, 16
    rows = images.reshape(count, 2, blocks, LANES).transpose(0, 2, 1, 3).reshape(count, 2 * blocks, LANES)
    height = 2 * blocks + COUNT_ROWS
    model = model_slice.reshape(2, blocks, LANES).transpose(1, 0, 2).reshape(2 * blocks, LANES)
    index = block_index[0].T
    return pl.pallas_call(
        functools.partial(sums_kernel, half, unroll, piece),
        in_specs=[HBM] * 6,
        out_specs=[VMEM] * 9,
        out_shape=[
            jax.ShapeDtypeStruct((bins, height, LANES), f32),
            jax.ShapeDtypeStruct((half, height, LANES), bf16),
        ]
        + [jax.ShapeDtypeStruct((n, blocks, LANES), f32) for n in (FINE, FINE, COARSE_USED, COARSE_USED)]
        + [
            jax.ShapeDtypeStruct((blocks, LANES), f32),
            jax.ShapeDtypeStruct(model.shape, f32),
            jax.ShapeDtypeStruct(index.shape, jnp.int32),
        ],
        scratch_shapes=[
            pltpu.SMEM((count,), jnp.int32),
            pltpu.VMEM((1, count), jnp.int32),
            pltpu.VMEM(rows.shape, bf16),
            pltpu.VMEM((1, count), bf16),
            pltpu.SMEM((count,), jnp.int32),
            pltpu.VMEM((1, count), jnp.int32),
            pltpu.SemaphoreType.DMA,
            pltpu.SemaphoreType.DMA((4,)),
            pltpu.SemaphoreType.DMA((count // piece,)),
            pltpu.SemaphoreType.DMA((2,)),
        ],
        compiler_params=pltpu.CompilerParams(vmem_limit_bytes=24 * 2**20),
    )(
        *in_hbm(
            [
                pose_bin.reshape(1, -1),
                rows,
                defocus.reshape(1, -1),
                freq_sq.reshape(blocks, LANES),
                model,
                index,
            ]
        )
    )


def turn_by(cosine, sine, by):
    return cosine * by[0] - sine * by[1], sine * by[0] + cosine * by[1]


def tables_kernel(fine_sin, fine_cos, coarse_sin, coarse_cos, freq, fine, coarse):
    blocks = freq.shape[0]
    first = lax.broadcasted_iota(jnp.int32, (8, LANES), 0).astype(f32)

    def entry(cosines, sines, k, n):
        rows = pl.ds(n * blocks + k, 1)
        return cosines[rows, :], sines[rows, :]

    def one(k):
        lanes = [pl.ds(pl.multiple_of((2 * k + part) * LANES, LANES), LANES) for part in range(2)]
        f = freq[pl.ds(k, 1), :]
        angle = first * (f * (0.125 / math.pi))
        pair = [cosine_and_sine(angle)]
        by = entry(fine_cos, fine_sin, k, 16)
        for _ in range(FINE // 8 - 1):
            pair.append(turn_by(*pair[-1], by))
        for part in range(2):
            fine[:, lanes[part]] = jnp.concatenate([p[part] for p in pair], axis=0).astype(bf16)
        angle = first * (f * (16.0 / math.pi))
        angle = angle - ((angle + ROUND) - ROUND)
        even = cosine_and_sine(angle)
        by = entry(coarse_cos, coarse_sin, k, 16)
        pair = [even, turn_by(*even, turn_by(*by, by))]
        by = entry(coarse_cos, coarse_sin, k, 2)
        pair += [turn_by(*p, by) for p in pair]
        coarse[:, lanes[0]] = jnp.concatenate([p[0] for p in pair], axis=0)
        coarse[:, lanes[1]] = jnp.concatenate([p[1] for p in pair], axis=0)

    def body(j, _):
        for k in range(GROUP):
            one(GROUP * j + k)
        return 0

    lax.fori_loop(0, blocks // GROUP, body, 0)


def tables(angles):
    blocks = angles[-1].shape[0]
    shapes = [((FINE, 2 * blocks * LANES), bf16), ((COARSE, 2 * blocks * LANES), f32)]
    return pl.pallas_call(
        tables_kernel,
        in_specs=[VMEM] * 5,
        out_specs=[VMEM] * 2,
        out_shape=[jax.ShapeDtypeStruct(shape, dtype) for shape, dtype in shapes],
        cost_estimate=pl.CostEstimate(flops=20 * 10**9, bytes_accessed=16 * 10**6, transcendentals=0),
        compiler_params=pltpu.CompilerParams(vmem_limit_bytes=8 * 2**20),
    )(*[a.reshape(-1, LANES) for a in angles])


def volume_kernel(
    scale, sums_ref, model_ref, index_ref, fine, coarse, coef_ref, out_ref, power, residual, terms
):
    blocks, touched = coef_ref.shape[:2]
    total = sums_ref[0].astype(f32)
    for part in range(1, sums_ref.shape[0]):
        total = total + sums_ref[part].astype(f32)
    counts = total[2 * blocks :]
    counts = jnp.concatenate([counts, pltpu.roll(counts, FINE, 1)], axis=0)[:, :FINE]
    named = jnp.sum(counts)
    high = counts.astype(bf16)
    counts = jnp.concatenate([high, (counts - high.astype(f32)).astype(bf16)], axis=0)
    for first in range(0, blocks, GROUP):
        lanes = slice(2 * first * LANES, 2 * (first + GROUP) * LANES)
        inner = jnp.dot(counts, fine[:, lanes], preferred_element_type=f32)
        cosine = (inner[:COARSE] + inner[COARSE:]) * coarse[:, lanes]
        cosine = sum(cosine[n : n + 8] for n in range(0, COARSE, 8))
        for k in range(GROUP):
            both = cosine[:, 2 * k * LANES : (2 * k + 1) * LANES] - cosine[:, (2 * k + 1) * LANES : (2 * k + 2) * LANES]
            both = jnp.sum(both, axis=0, keepdims=True)
            power[first + k : first + k + 1, :] = (named - both) * 0.5

    for c in range(2):
        model = model_ref[pl.ds(c, blocks, 2), :]
        residual[c] = (power[...] * model - total[c * blocks : (c + 1) * blocks]) * scale

    row = lax.broadcasted_iota(jnp.int32, (GROUP, LANES), 0)
    for first in range(0, blocks, GROUP):
        left = jnp.concatenate(
            [
                jnp.concatenate(
                    [jnp.where(row == m, residual[c, first : first + GROUP], 0.0) for m in range(GROUP)],
                    axis=1,
                )
                for c in range(2)
            ],
            axis=0,
        ).astype(bf16)
        for j in range(touched):
            right = coef_ref[first : first + GROUP, j].reshape(GROUP * LANES, LANES)
            got = jnp.dot(left, right, preferred_element_type=f32)
            for c in range(2):
                terms[j, first : first + GROUP, c * LANES : (c + 1) * LANES] = got[c * GROUP : (c + 1) * GROUP]

    volume = out_ref.shape[0]
    rows = lax.broadcasted_iota(jnp.int32, (volume, blocks), 0)
    total = jnp.zeros(out_ref.shape, f32)
    for j in range(touched):
        onehot = jnp.where(rows == index_ref[pl.ds(j, 1), :], 1.0, 0.0).astype(bf16)
        whole = terms[j]
        for _ in range(2):
            piece = whole.astype(bf16)
            whole = whole - piece.astype(f32)
            total = total + jnp.dot(onehot, piece, preferred_element_type=f32)
    out_ref[...] = total


def volume_share(sums, loaded, coef, volume, scale):
    blocks, touched = coef.shape[:2]
    return pl.pallas_call(
        functools.partial(volume_kernel, scale),
        in_specs=[VMEM] * 6,
        out_specs=VMEM,
        out_shape=jax.ShapeDtypeStruct((volume, 2 * LANES), f32),
        scratch_shapes=[
            pltpu.VMEM((blocks, LANES), f32),
            pltpu.VMEM((2, blocks, LANES), f32),
            pltpu.VMEM((touched, blocks, 2 * LANES), f32),
        ],
        compiler_params=pltpu.CompilerParams(vmem_limit_bytes=16 * 2**20),
    )(sums, *loaded, coef)


def shards(images, defocus, pose_bin, freq_sq, model_slice, interp_coef, block_index, volume):
    slabs = lax.axis_size("slab")
    shells = lax.axis_size("shell")
    kept, other, *angles, model, index = weighted_sums(
        images, defocus, pose_bin, freq_sq, model_slice, block_index, slabs
    )
    loaded = [model, index, *tables(angles)]
    other = lax.ppermute(other, "slab", [(i, i ^ 1) for i in range(slabs)])
    half = slabs // 2
    pair = (kept[:half] + other.astype(f32)).astype(bf16)
    pair, loaded = lax.optimization_barrier((pair, loaded))
    sums = lax.all_to_all(
        pair,
        "slab",
        split_axis=0,
        concat_axis=0,
        tiled=True,
        axis_index_groups=[list(range(side, slabs, 2)) for side in range(2)],
    )
    share = volume_share(sums, loaded, interp_coef[0], volume, 1.0 / images.shape[0])
    owned = volume // (slabs * shells)
    shares = lax.all_to_all(share, ("slab", "shell"), split_axis=0, concat_axis=0, tiled=True)
    return jnp.sum(shares.reshape(slabs * shells, owned, 2, LANES), axis=0)


def solution(mesh):
    owned = 4
    volume = owned * mesh.shape["slab"] * mesh.shape["shell"]
    return jax.shard_map(
        functools.partial(shards, volume=volume),
        mesh=mesh,
        in_specs=(
            P("slab", None, "shell"),
            P("slab"),
            P("slab", None),
            P("shell"),
            P("slab", None, "shell"),
            P("slab", "shell", None, None, None),
            P("slab", "shell", None),
        ),
        out_specs=P(("slab", "shell"), None, None),
        check_vma=False,
    )
```

```python
import functools
import math

import jax
import jax.numpy as jnp
import numpy as np
from jax import lax
from jax.experimental import pallas as pl
from jax.experimental.pallas import tpu as pltpu
from jax.sharding import PartitionSpec as P

f32 = jnp.float32
bf16 = jnp.bfloat16
LANES = 128
GROUP = 8
LEAD = 2
FINE = 64
COARSE = 32
COARSE_USED = 26
COUNT_ROWS = 16
ROUND = 12582912.0


HBM = pl.BlockSpec(memory_space=pltpu.HBM)
VMEM = pl.BlockSpec(memory_space=pltpu.VMEM)


def sine_coefficients():
    x = np.cos(np.pi * (np.arange(400) + 0.5) / 400)
    cheb = np.polynomial.chebyshev.Chebyshev.fit(x, np.sin(np.pi * x), 11, domain=[-1, 1])
    power = cheb.convert(kind=np.polynomial.Polynomial).coef
    return [float(power[2 * n + 1] * 2.0 ** (2 * n + 1)) for n in range(6)]


SINE = sine_coefficients()


def cosine_coefficients():
    x = np.cos(np.pi * (np.arange(400) + 0.5) / 400)
    cheb = np.polynomial.chebyshev.Chebyshev.fit(x, np.cos(np.pi * x), 12, domain=[-1, 1])
    power = cheb.convert(kind=np.polynomial.Polynomial).coef
    return [float(power[2 * n] * 4.0**n) for n in range(7)]


COSINE = cosine_coefficients()


def horner(coefficients, q):
    value = q * coefficients[-1] + coefficients[-2]
    for c in coefficients[-3::-1]:
        value = value * q + c
    return value


def cosine_and_sine(r):
    q = r * r
    return horner(COSINE, q), horner(SINE, q) * r


def sine_of_turns(turns):
    r = turns - ((turns + ROUND) - ROUND)
    q = r * r
    s = q * SINE[5] + SINE[4]
    for n in (3, 2, 1, 0):
        s = s * q + SINE[n]
    return s * r


def in_hbm(arrays):
    return [pltpu.with_memory_space_constraint(a, pltpu.HBM) for a in arrays]


def fill_table(sines, cosines, turns):
    count = sines.shape[0]
    sines[0] = jnp.zeros_like(turns)
    cosines[0] = jnp.ones_like(turns)
    sines[1] = sine_of_turns(turns)
    cosines[1] = sine_of_turns(turns + 0.25)
    done = 2
    while done < count:
        last = done - 1
        s, c = sines[last], cosines[last]
        for n in range(1, min(done, count - last)):
            sines[last + n] = s * cosines[n] + c * sines[n]
            cosines[last + n] = c * cosines[n] - s * sines[n]
        done += min(done, count - last) - 1


def sums_kernel(
    half,
    unroll,
    piece,
    pose_hbm,
    images_hbm,
    defocus_hbm,
    freq_hbm,
    model_hbm,
    index_hbm,
    kept_ref,
    other_ref,
    fine_sin,
    fine_cos,
    coarse_sin,
    coarse_cos,
    freq,
    model,
    index,
    pose,
    pose_row,
    images,
    defocus,
    steps,
    step_row,
    step_sem,
    small_sems,
    image_sems,
    late_sems,
):
    count = images.shape[0]
    blocks = freq.shape[0]
    small = [
        pltpu.make_async_copy(src, dst, small_sems.at[n])
        for n, (src, dst) in enumerate(
            ((freq_hbm, freq), (defocus_hbm, defocus), (pose_hbm, pose_row), (pose_hbm.at[0], pose))
        )
    ]
    for copy in small:
        copy.start()

    def image_copy(j):
        rows = pl.ds(j * piece, piece)
        return pltpu.make_async_copy(images_hbm.at[rows], images.at[rows], image_sems.at[j])

    lead = min(LEAD, count // piece)
    for j in range(lead):
        image_copy(j).start()
    kept_ref[...] = jnp.zeros_like(kept_ref)
    rows = lax.broadcasted_iota(jnp.int32, (2 * blocks, 2 * blocks), 0)
    cols = lax.broadcasted_iota(jnp.int32, (2 * blocks, 2 * blocks), 1)
    apart = jnp.where(cols == 2 * (rows % blocks) + rows // blocks, 1.0, 0.0).astype(bf16)
    for copy in small[:2]:
        copy.wait()
    for j in range(lead, count // piece):
        image_copy(j).start()
    late = [
        pltpu.make_async_copy(src, dst, late_sems.at[n])
        for n, (src, dst) in enumerate(((model_hbm, model), (index_hbm, index)))
    ]
    for copy in late:
        copy.start()
    side = lax.axis_index("slab") & 1
    step_row[...] = (defocus[...].astype(f32) * 8.0).astype(jnp.int32)
    step_copy = pltpu.make_async_copy(step_row.at[0], steps, step_sem)
    step_copy.start()
    fill_table(fine_sin, fine_cos, freq[...] * (0.0625 / math.pi))
    fill_table(coarse_sin, coarse_cos, freq[...] * (4.0 / math.pi))
    for copy in small[2:]:
        copy.wait()
    bins = 2 * half
    place = ((pose_row[...] & 1) ^ side) * half + (pose_row[...] >> 1)
    place = place * COUNT_ROWS + (step_row[...] >> 7)
    chosen = lax.broadcasted_iota(jnp.int32, (bins * COUNT_ROWS, count), 0) == place
    chosen = jnp.where(chosen, 1.0, 0.0).astype(bf16)
    named = lax.broadcasted_iota(jnp.int32, (LANES, count), 0) == (step_row[...] & (LANES - 1))
    named = jnp.where(named, 1.0, 0.0).astype(bf16)
    numbers = lax.dot_general(chosen, named, (((1,), (1,)), ((), ())), preferred_element_type=f32)
    kept_ref[:, 2 * blocks :] = numbers.reshape(bins, COUNT_ROWS, LANES)
    step_copy.wait()

    def one(image):
        u, v = steps[image] >> 6, steps[image] & (FINE - 1)
        s = coarse_sin[u] * fine_cos[v] + coarse_cos[u] * fine_sin[v]
        both = jnp.dot(apart, images[image], preferred_element_type=f32)
        bin_ = pose[image]
        slot = ((bin_ & 1) ^ side) * half + (bin_ >> 1)
        return slot, s, both

    def body(j, _):
        for k in range(unroll // piece):
            image_copy(j * (unroll // piece) + k).wait()
        for k in range(unroll):
            slot, s, both = one(unroll * j + k)
            for part, value in enumerate((s * both[:blocks], s * both[blocks:])):
                kept_ref[slot, part * blocks : (part + 1) * blocks] += value
        return 0

    lax.fori_loop(0, count // unroll, body, 0)
    other_ref[...] = kept_ref[half:].astype(other_ref.dtype)
    for copy in late:
        copy.wait()


def weighted_sums(images, defocus, pose_bin, freq_sq, model_slice, block_index, bins):
    count, _, width = images.shape
    blocks = width // LANES
    half = bins // 2
    unroll, piece = 32, 16
    rows = images.reshape(count, 2, blocks, LANES).transpose(0, 2, 1, 3).reshape(count, 2 * blocks, LANES)
    height = 2 * blocks + COUNT_ROWS
    model = model_slice.reshape(2, blocks, LANES).transpose(1, 0, 2).reshape(2 * blocks, LANES)
    index = block_index[0].T
    return pl.pallas_call(
        functools.partial(sums_kernel, half, unroll, piece),
        in_specs=[HBM] * 6,
        out_specs=[VMEM] * 9,
        out_shape=[
            jax.ShapeDtypeStruct((bins, height, LANES), f32),
            jax.ShapeDtypeStruct((half, height, LANES), bf16),
        ]
        + [jax.ShapeDtypeStruct((n, blocks, LANES), f32) for n in (FINE, FINE, COARSE_USED, COARSE_USED)]
        + [
            jax.ShapeDtypeStruct((blocks, LANES), f32),
            jax.ShapeDtypeStruct(model.shape, f32),
            jax.ShapeDtypeStruct(index.shape, jnp.int32),
        ],
        scratch_shapes=[
            pltpu.SMEM((count,), jnp.int32),
            pltpu.VMEM((1, count), jnp.int32),
            pltpu.VMEM(rows.shape, bf16),
            pltpu.VMEM((1, count), bf16),
            pltpu.SMEM((count,), jnp.int32),
            pltpu.VMEM((1, count), jnp.int32),
            pltpu.SemaphoreType.DMA,
            pltpu.SemaphoreType.DMA((4,)),
            pltpu.SemaphoreType.DMA((count // piece,)),
            pltpu.SemaphoreType.DMA((2,)),
        ],
        compiler_params=pltpu.CompilerParams(vmem_limit_bytes=24 * 2**20),
    )(
        *in_hbm(
            [
                pose_bin.reshape(1, -1),
                rows,
                defocus.reshape(1, -1),
                freq_sq.reshape(blocks, LANES),
                model,
                index,
            ]
        )
    )


def turn_by(cosine, sine, by):
    return cosine * by[0] - sine * by[1], sine * by[0] + cosine * by[1]


def tables_kernel(fine_sin, fine_cos, coarse_sin, coarse_cos, freq, fine, coarse):
    blocks = freq.shape[0]
    first = lax.broadcasted_iota(jnp.int32, (8, LANES), 0).astype(f32)

    def entry(cosines, sines, k, n):
        rows = pl.ds(n * blocks + k, 1)
        return cosines[rows, :], sines[rows, :]

    def one(k):
        lanes = [pl.ds(pl.multiple_of((2 * k + part) * LANES, LANES), LANES) for part in range(2)]
        f = freq[pl.ds(k, 1), :]
        angle = first * (f * (0.125 / math.pi))
        pair = [cosine_and_sine(angle)]
        by = entry(fine_cos, fine_sin, k, 16)
        for _ in range(FINE // 8 - 1):
            pair.append(turn_by(*pair[-1], by))
        for part in range(2):
            fine[:, lanes[part]] = jnp.concatenate([p[part] for p in pair], axis=0).astype(bf16)
        angle = first * (f * (16.0 / math.pi))
        angle = angle - ((angle + ROUND) - ROUND)
        even = cosine_and_sine(angle)
        by = entry(coarse_cos, coarse_sin, k, 16)
        pair = [even, turn_by(*even, turn_by(*by, by))]
        by = entry(coarse_cos, coarse_sin, k, 2)
        pair += [turn_by(*p, by) for p in pair]
        coarse[:, lanes[0]] = jnp.concatenate([p[0] for p in pair], axis=0)
        coarse[:, lanes[1]] = jnp.concatenate([p[1] for p in pair], axis=0)

    def body(j, _):
        for k in range(GROUP):
            one(GROUP * j + k)
        return 0

    lax.fori_loop(0, blocks // GROUP, body, 0)


def tables(angles):
    blocks = angles[-1].shape[0]
    shapes = [((FINE, 2 * blocks * LANES), bf16), ((COARSE, 2 * blocks * LANES), f32)]
    return pl.pallas_call(
        tables_kernel,
        in_specs=[VMEM] * 5,
        out_specs=[VMEM] * 2,
        out_shape=[jax.ShapeDtypeStruct(shape, dtype) for shape, dtype in shapes],
        cost_estimate=pl.CostEstimate(flops=20 * 10**9, bytes_accessed=16 * 10**6, transcendentals=0),
        compiler_params=pltpu.CompilerParams(vmem_limit_bytes=8 * 2**20),
    )(*[a.reshape(-1, LANES) for a in angles])


def volume_kernel(
    scale, sums_ref, model_ref, index_ref, fine, coarse, coef_ref, out_ref, power, residual, terms
):
    blocks, touched = coef_ref.shape[:2]
    total = sums_ref[0].astype(f32)
    for part in range(1, sums_ref.shape[0]):
        total = total + sums_ref[part].astype(f32)
    counts = total[2 * blocks :]
    counts = jnp.concatenate([counts, pltpu.roll(counts, FINE, 1)], axis=0)[:, :FINE]
    named = jnp.sum(counts)
    high = counts.astype(bf16)
    counts = jnp.concatenate([high, (counts - high.astype(f32)).astype(bf16)], axis=0)
    for first in range(0, blocks, GROUP):
        lanes = slice(2 * first * LANES, 2 * (first + GROUP) * LANES)
        inner = jnp.dot(counts, fine[:, lanes], preferred_element_type=f32)
        cosine = (inner[:COARSE] + inner[COARSE:]) * coarse[:, lanes]
        cosine = sum(cosine[n : n + 8] for n in range(0, COARSE, 8))
        for k in range(GROUP):
            both = cosine[:, 2 * k * LANES : (2 * k + 1) * LANES] - cosine[:, (2 * k + 1) * LANES : (2 * k + 2) * LANES]
            both = jnp.sum(both, axis=0, keepdims=True)
            power[first + k : first + k + 1, :] = (named - both) * 0.5

    for c in range(2):
        model = model_ref[pl.ds(c, blocks, 2), :]
        residual[c] = (power[...] * model - total[c * blocks : (c + 1) * blocks]) * scale

    row = lax.broadcasted_iota(jnp.int32, (GROUP, LANES), 0)
    for first in range(0, blocks, GROUP):
        left = jnp.concatenate(
            [
                jnp.concatenate(
                    [jnp.where(row == m, residual[c, first : first + GROUP], 0.0) for m in range(GROUP)],
                    axis=1,
                )
                for c in range(2)
            ],
            axis=0,
        ).astype(bf16)
        for j in range(touched):
            right = coef_ref[first : first + GROUP, j].reshape(GROUP * LANES, LANES)
            got = jnp.dot(left, right, preferred_element_type=f32)
            for c in range(2):
                terms[j, first : first + GROUP, c * LANES : (c + 1) * LANES] = got[c * GROUP : (c + 1) * GROUP]

    volume = out_ref.shape[0]
    rows = lax.broadcasted_iota(jnp.int32, (volume, blocks), 0)
    total = jnp.zeros(out_ref.shape, f32)
    for j in range(touched):
        onehot = jnp.where(rows == index_ref[pl.ds(j, 1), :], 1.0, 0.0).astype(bf16)
        whole = terms[j]
        for _ in range(2):
            piece = whole.astype(bf16)
            whole = whole - piece.astype(f32)
            total = total + jnp.dot(onehot, piece, preferred_element_type=f32)
    out_ref[...] = total


def volume_share(sums, loaded, coef, volume, scale):
    blocks, touched = coef.shape[:2]
    return pl.pallas_call(
        functools.partial(volume_kernel, scale),
        in_specs=[VMEM] * 6,
        out_specs=VMEM,
        out_shape=jax.ShapeDtypeStruct((volume, 2 * LANES), f32),
        scratch_shapes=[
            pltpu.VMEM((blocks, LANES), f32),
            pltpu.VMEM((2, blocks, LANES), f32),
            pltpu.VMEM((touched, blocks, 2 * LANES), f32),
        ],
        compiler_params=pltpu.CompilerParams(vmem_limit_bytes=16 * 2**20),
    )(sums, *loaded, coef)


def shards(images, defocus, pose_bin, freq_sq, model_slice, interp_coef, block_index, volume):
    slabs = lax.axis_size("slab")
    shells = lax.axis_size("shell")
    kept, other, *angles, model, index = weighted_sums(
        images, defocus, pose_bin, freq_sq, model_slice, block_index, slabs
    )
    loaded = [model, index, *tables(angles)]
    other = lax.ppermute(other, "slab", [(i, i ^ 1) for i in range(slabs)])
    half = slabs // 2
    pair = (kept[:half] + other.astype(f32)).astype(bf16)
    pair, loaded = lax.optimization_barrier((pair, loaded))
    sums = lax.all_to_all(
        pair,
        "slab",
        split_axis=0,
        concat_axis=0,
        tiled=True,
        axis_index_groups=[list(range(side, slabs, 2)) for side in range(2)],
    )
    share = volume_share(sums, loaded, interp_coef[0], volume, 1.0 / images.shape[0])
    owned = volume // (slabs * shells)
    shares = lax.all_to_all(share, ("slab", "shell"), split_axis=0, concat_axis=0, tiled=True)
    return jnp.sum(shares.reshape(slabs * shells, owned, 2, LANES), axis=0)


def solution(mesh):
    owned = 4
    volume = owned * mesh.shape["slab"] * mesh.shape["shell"]
    return jax.shard_map(
        functools.partial(shards, volume=volume),
        mesh=mesh,
        in_specs=(
            P("slab", None, "shell"),
            P("slab"),
            P("slab", None),
            P("shell"),
            P("slab", None, "shell"),
            P("slab", "shell", None, None, None),
            P("slab", "shell", None),
        ),
        out_specs=P(("slab", "shell"), None, None),
        check_vma=False,
    )
```
